256 devices in a mesh: prow: 16 (over z, core), pcol: 16 (over y, x).
Axes of the slice: x: 4, y: 4, z: 8, core: 2. Of those that a mesh axis runs over, the one named last changes fastest.
Arguments:
- panel_pre: bfloat16 [31, 16, 256, 1, 16, 256], P(None, 'prow', None, None, 'pcol'), may hold values from -0.015625 to 0.015625
- tail_panel: bfloat16 [1, 16, 256, 1, 16, 256], P(None, 'prow', None, None, 'pcol'), may hold values from -0.09375 to 0.09375
- earlier: bfloat16 [32, 31, 16, 256], P('pcol', None, 'prow'), may hold values from -6 to 6
- right_side: float32 [32, 1, 16, 256], P(None, None, 'pcol'), may hold values from -6 to 6
- inverses: float32 [1, 16, 256, 1024], P(None, 'pcol'), may hold values from -0.08 to 1.08
Outputs:
- solution: float32 [32, 1, 16, 256], P(None, None, 'pcol')
The draws below stay inside these ranges and needn't reach their ends.
All inputs are finite; a program needn't handle non-finite values.
Results may differ from the reference program's by a relative error of at most 0.0021.
Values may be sent and summed in bfloat16 or wider, within the bound.
A program may use at most 64 MiB of HBM per device.

```python
import jax
import jax.numpy as jnp
from jax import lax

ORDER = 131072
NB = 1024
TILE = 256
STEPS = 4
NRHS = 32
COLS = 4096
PRE = 126976
GR = 16
GC = 16
CRP = 31
CT = 1
CC = 1


def draw_inverses(key, part):
    key = jax.random.fold_in(key, 7)
    tile_turn = jnp.arange(CC, dtype=jnp.int32)[:, None, None]
    owner = jnp.arange(GC, dtype=jnp.int32)[None, :, None]
    inside = jnp.arange(TILE, dtype=jnp.int32)[None, None, :]
    rows = ((tile_turn * GC + owner) * TILE + inside) % NB
    unit = (rows[..., None] == jnp.arange(NB, dtype=jnp.int32)).astype(jnp.float32)
    spread = 0.6 / NB ** 0.5
    noise = jnp.clip(jax.random.normal(key, (CC, GC, TILE, NB), jnp.float32), -4.0, 4.0) * spread
    noise = jnp.clip(noise, -0.075, 0.075)
    return unit + noise


def levels(stream_key, extent, split, least, largest):
    def one(dim, shards_of):
        steps = jax.random.uniform(jax.random.fold_in(jax.random.fold_in(stream_key, 6), dim), (shards_of,), jnp.float32, least / len(split), largest / len(split))
        return jnp.repeat(jnp.exp(steps), extent[dim] // shards_of).reshape((-1,) + (1,) * (len(extent) - dim - 1))

    level = one(*split[0])
    for cut in split[1:]:
        level = level * one(*cut)
    return level


def normal_values(own_key, extent, scale, limit, pieces=(), kind=jnp.bfloat16):
    loudness = levels(own_key, extent, pieces, -0.22, 0.18) if pieces else 1.0
    array = jax.random.normal(own_key, extent, jnp.float32) * scale * loudness
    return jnp.minimum(jnp.maximum(array, -limit), limit).astype(kind)


def setup_inputs(seed: int = 0) -> dict:
    streams_of = jax.random.split(jax.random.key(seed), 6)
    return {
        "panel_pre": normal_values(streams_of[0], (CRP, GR, TILE, CC, GC, TILE), ORDER ** -0.5, 0.015625, ((1, 16), (4, 16))),
        "tail_panel": normal_values(streams_of[1], (CT, GR, TILE, CC, GC, TILE), COLS ** -0.5, 0.09375, ((1, 16), (4, 16))),
        "earlier": normal_values(streams_of[2], (NRHS, CRP, GR, TILE), 1.0, 6.0, ((0, 16), (2, 16))),
        "right_side": normal_values(streams_of[3], (NRHS, CC, GC, TILE), 1.0, 6.0, ((2, 16),), jnp.float32),
        "inverses": draw_inverses(jax.random.fold_in(streams_of[5], 71), 0),
    }


def reference(panel_pre, tail_panel, earlier, right_side, inverses):
    mat_pre = panel_pre.reshape(PRE, COLS)
    mat_tail = tail_panel.reshape(COLS, COLS)
    known = earlier.reshape(NRHS, PRE)
    rhs_flat = right_side.reshape(NRHS, COLS)
    inv_flat = inverses.reshape(COLS, NB)
    prior = jnp.dot(known, mat_pre, preferred_element_type=jnp.float32)
    solved = jnp.zeros((NRHS, COLS), jnp.float32)
    for step in range(STEPS):
        first = step * NB
        rounded = solved.astype(jnp.bfloat16)
        update = jnp.dot(rounded, mat_tail[:, first:first + NB], preferred_element_type=jnp.float32)
        remain = (rhs_flat[:, first:first + NB] - prior[:, first:first + NB]) - update
        block_x = jnp.dot(remain, inv_flat[first:first + NB, :], precision=lax.Precision.HIGHEST)
        solved = solved.at[:, first:first + NB].set(block_x)
    return solved.reshape(NRHS, CC, GC, TILE)
```

```python
import functools

import jax
import jax.numpy as jnp
from jax import lax
from jax.experimental import pallas as pl
from jax.experimental.pallas import tpu as pltpu
from jax.sharding import PartitionSpec as P

MESH = pl.DeviceIdType.MESH
F32 = jnp.float32
BF16 = jnp.bfloat16
CHUNKS = 4


def kernel(a_hbm, b_hbm, e_hbm, r_hbm, g_hbm, o_ref, e_ref, r_ref, abuf, ball, gbuf, h, part, pin, cxs, cxd, gp, xin, oin, ob, lsem, ysem, bsend, brecv, psem, csem, xsend, xrecv, osem, fsem):
    p = lax.axis_index("prow")
    col = lax.axis_index("pcol")
    z, core = p // 2, p % 2
    y, x = col // 4, col % 4
    turns = abuf.shape[0]

    def both(ref, sem):
        return pltpu.make_async_copy(ref, ref, sem)

    step = -(-turns // CHUNKS)
    loads = []
    for i in range(CHUNKS):
        size = min(step, turns - i * step)
        loads.append(pltpu.make_async_copy(a_hbm.at[pl.ds(i * step, size)], abuf.at[pl.ds(i * step, size)], lsem.at[i]))
    gload = [
        pltpu.make_async_copy(g_hbm.at[:, pl.ds(pl.multiple_of((core + 2 * i) * 256, 256), 256)], gbuf.at[i], lsem.at[CHUNKS + i])
        for i in range(2)
    ]
    load_y = pltpu.make_async_copy(e_hbm, e_ref, lsem.at[CHUNKS + 4])
    load_r = pltpu.make_async_copy(r_hbm.at[z], r_ref, lsem.at[CHUNKS + 5])
    own_y = pltpu.make_async_copy(e_hbm, h.at[:, col], lsem.at[CHUNKS + 2])
    own_b = pltpu.make_async_copy(b_hbm, ball.at[z], lsem.at[CHUNKS + 3])
    load_y.start()
    own_y.start()
    for c in loads:
        c.start()
    for c in gload:
        c.start()

    @pl.when(z < 2 * y)
    def _():
        own_b.start()

    load_r.start()

    cxs[...] = jnp.zeros_like(cxs)
    cxd[...] = jnp.zeros_like(cxd)

    barrier = pltpu.get_barrier_semaphore()
    for d in range(1, 16):
        pl.semaphore_signal(barrier, inc=1, device_id=(p, (col + d) % 16), device_id_type=MESH)
        pl.semaphore_signal(barrier, inc=1, device_id=((p + d) % 16, col), device_id_type=MESH)
    pl.semaphore_wait(barrier, 30)
    load_y.wait()

    for d in range(1, 16):
        pltpu.make_async_remote_copy(
            e_ref, h.at[:, col], ysem.at[0], ysem.at[1], device_id=(p, (col + d) % 16), device_id_type=MESH
        ).start()

    @pl.when(z < 2 * y)
    def _():
        for d in range(1, 8):
            pltpu.make_async_remote_copy(
                b_hbm, ball.at[z], bsend.at[0], brecv.at[z], device_id=((p + 2 * d) % 16, col), device_id_type=MESH
            ).start()

    own_y.wait()
    both(h.at[:, pl.ds(0, 15)], ysem.at[1]).wait()
    acc = jnp.zeros((32, 256), F32)
    for i in range(CHUNKS):
        loads[i].wait()
        for t in range(i * step, min((i + 1) * step, turns)):
            lhs = jnp.concatenate([h[2 * t].reshape(32, 128), h[2 * t + 1].reshape(32, 128)], axis=1)
            acc += jnp.dot(lhs, abuf[t], preferred_element_type=F32)
    part[...] = acc.reshape(8, 4, 256)

    for d in range(1, 16):
        to = (p + d) % 16
        pltpu.make_async_remote_copy(
            part.at[to // 2], pin.at[p], psem.at[0], psem.at[1], device_id=(to, col), device_id_type=MESH
        ).start()
    pin[p] = part[z]
    load_r.wait()
    rhs = r_ref[...].reshape(4, 256)
    both(pin.at[pl.ds(0, 15)], psem.at[1]).wait()
    base = rhs - jnp.sum(pin[...], axis=0)


    for i in range(3):

        @pl.when(y > i)
        def _():
            for k in range(2):

                @pl.when(z == 2 * i + k)
                def _():
                    own_b.wait()

                @pl.when(z != 2 * i + k)
                def _():
                    both(ball.at[2 * i + k], brecv.at[2 * i + k]).wait()

            both(xin.at[i], xrecv.at[i]).wait()
            solved = jnp.sum(xin[i], axis=0).astype(BF16)
            upd = cxs[...]
            for k in range(2):
                upd += jnp.dot(solved[k], ball[2 * i + k], preferred_element_type=F32)
            cxs[...] = upd

    @pl.when(y > 0)
    def _():
        swap = pltpu.make_async_remote_copy(
            cxs, cxd, csem.at[0], csem.at[1], device_id=(p + 1 - 2 * core, col), device_id_type=MESH
        )
        swap.start()
        swap.wait()

    update = cxs[...] + cxd[...]
    remain = base - update
    for i in range(2):
        gload[i].wait()
        gp[i] = jnp.dot(remain, gbuf[i], precision=lax.Precision.HIGHEST)

    for j in range(1, 4):

        @pl.when(y < j)
        def _():
            for k in range(4):
                pltpu.make_async_remote_copy(
                    gp, xin.at[y, x], xsend.at[j], xrecv.at[y], device_id=(p, 4 * j + k), device_id_type=MESH
                ).start()

    for k in range(2):
        to = core + 2 * k

        @pl.when(to != x)
        def _():
            pltpu.make_async_remote_copy(
                gp.at[k], oin.at[x], osem.at[k], osem.at[2], device_id=(p, 4 * y + to), device_id_type=MESH
            ).start()

    mine = x % 2 == core

    @pl.when(mine)
    def _():
        oin[x] = gp[x // 2]
        both(oin.at[pl.ds(0, 3)], osem.at[2]).wait()
        total = jnp.sum(oin[...], axis=0).reshape(4, 1, 256)
        ob[...] = total
        for d in range(1, 16):
            pltpu.make_async_remote_copy(
                ob, o_ref.at[z], fsem.at[0], fsem.at[1], device_id=((p + d) % 16, col), device_id_type=MESH
            ).start()
        o_ref[z] = total
        both(o_ref.at[pl.ds(0, 7)], fsem.at[1]).wait()
        both(o_ref.at[pl.ds(0, 7)], fsem.at[0]).wait()
        both(o_ref.at[pl.ds(0, 8)], fsem.at[0]).wait()

    @pl.when(jnp.logical_not(mine))
    def _():
        both(o_ref, fsem.at[1]).wait()

    both(h.at[:, pl.ds(0, 15)], ysem.at[0]).wait()
    both(pin.at[pl.ds(0, 15)], psem.at[0]).wait()

    @pl.when(z < 2 * y)
    def _():
        both(ball.at[pl.ds(0, 6)], bsend.at[0]).wait()
        both(ball.at[0], bsend.at[0]).wait()

        @pl.when(z >= 6)
        def _():
            own_b.wait()

    for j in range(1, 4):

        @pl.when(y < j)
        def _():
            both(xin.at[0], xsend.at[j]).wait()

    for k in range(2):

        @pl.when(core + 2 * k != x)
        def _():
            both(gp.at[k], osem.at[k]).wait()


def local(panel_pre, tail_panel, earlier, right_side, inverses):
    turns = panel_pre.shape[0]
    a = panel_pre.reshape(turns, 256, 256)
    b = tail_panel.reshape(256, 256)
    e = earlier.reshape(2, turns, 2, 128).transpose(1, 2, 0, 3).reshape(2 * turns, 2, 128)
    r = right_side.reshape(8, 4, 1, 256)
    g = inverses.reshape(256, 1024)
    hbm = pl.BlockSpec(memory_space=pltpu.HBM)
    vmem = pl.BlockSpec(memory_space=pltpu.VMEM)
    dma = pltpu.SemaphoreType.DMA
    out = pl.pallas_call(
        kernel,
        out_shape=jax.ShapeDtypeStruct((8, 4, 1, 256), F32),
        in_specs=[hbm] * 5,
        out_specs=vmem,
        scratch_shapes=[
            pltpu.VMEM((2 * turns, 2, 128), BF16),
            pltpu.VMEM((4, 1, 256), F32),
            pltpu.VMEM((turns, 256, 256), BF16),
            pltpu.VMEM((6, 256, 256), BF16),
            pltpu.VMEM((2, 256, 256), F32),
            pltpu.VMEM((2 * turns, 16, 2, 128), BF16),
            pltpu.VMEM((8, 4, 256), F32),
            pltpu.VMEM((16, 4, 256), F32),
            pltpu.VMEM((4, 256), F32),
            pltpu.VMEM((4, 256), F32),
            pltpu.VMEM((2, 4, 256), F32),
            pltpu.VMEM((3, 4, 2, 4, 256), F32),
            pltpu.VMEM((4, 4, 256), F32),
            pltpu.VMEM((4, 1, 256), F32),
            dma((CHUNKS + 6,)),
            dma((2,)),
            dma((1,)),
            dma((6,)),
            dma((2,)),
            dma((2,)),
            dma((4,)),
            dma((3,)),
            dma((3,)),
            dma((2,)),
        ],
        compiler_params=pltpu.CompilerParams(collective_id=0, has_side_effects=True, vmem_limit_bytes=64 << 20),
        cost_estimate=pl.CostEstimate(flops=2 * 32 * 256 * 256 * turns, bytes_accessed=6 << 20, transcendentals=0),
        name="solve",
    )(a, b, e, r, g)
    return out.reshape(32, 1, 1, 256)


def solution(mesh):
    in_specs = (
        P(None, "prow", None, None, "pcol", None),
        P(None, "prow", None, None, "pcol", None),
        P("pcol", None, "prow", None),
        P(None, None, "pcol", None),
        P(None, "pcol", None, None),
    )
    out_specs = P(None, None, "pcol", None)
    return jax.shard_map(local, mesh=mesh, in_specs=in_specs, out_specs=out_specs, check_vma=False)
```

```python
import jax
import jax.numpy as jnp
from jax import lax
from jax.experimental import pallas as pl
from jax.experimental.pallas import tpu as pltpu
from jax.sharding import PartitionSpec as P

MESH = pl.DeviceIdType.MESH
F32 = jnp.float32
BF16 = jnp.bfloat16
SPLIT = (0, 16, 31)


def kernel(a_hbm, b_hbm, e_hbm, r_hbm, g_hbm, o_ref, e_ref, r_ref, abuf, ball, gbuf, ghl, h, part, pin, upd, gp, xin, oin, ob, lsem, ysend, yrecv, bsend, brecv, psem, xsend, xrecv, osem, fsem):
    p = lax.axis_index("prow")
    col = lax.axis_index("pcol")
    z, core = p // 2, p % 2
    y, x = col // 4, col % 4
    solver = core == 1

    def both(ref, sem):
        return pltpu.make_async_copy(ref, ref, sem)

    def send(src, dst, ssem, rsem, to):
        pltpu.make_async_remote_copy(src, dst, ssem, rsem, device_id=to, device_id_type=MESH).start()

    load_y = pltpu.make_async_copy(e_hbm, e_ref, lsem.at[0])
    own_y = pltpu.make_async_copy(e_hbm, h.at[:, col], lsem.at[1])
    load_r = pltpu.make_async_copy(r_hbm.at[z], r_ref, lsem.at[2])
    load_g = pltpu.make_async_copy(g_hbm, gbuf, lsem.at[3])
    own_b = pltpu.make_async_copy(b_hbm, ball.at[p], lsem.at[4])
    chunks = [pl.ds(s, e - s) for s, e in zip(SPLIT, SPLIT[1:])]
    loads = [pltpu.make_async_copy(a_hbm.at[c], abuf.at[c], lsem.at[5 + i]) for i, c in enumerate(chunks)]
    has_b = p < 4 * y

    load_y.start()
    own_y.start()
    loads[0].start()

    @pl.when(solver)
    def _():
        load_g.start()
        load_r.start()

        @pl.when(has_b)
        def _():
            own_b.start()

    loads[1].start()

    barrier = pltpu.get_barrier_semaphore()
    for d in range(1, 16):
        pl.semaphore_signal(barrier, inc=1, device_id=(p, (col + d) % 16), device_id_type=MESH)
        pl.semaphore_signal(barrier, inc=1, device_id=((p + d) % 16, col), device_id_type=MESH)
    load_y.wait()
    pl.semaphore_wait(barrier, 30)

    for yy in range(4):
        for i, (s, e) in enumerate(zip(SPLIT, SPLIT[1:])):
            rows = pl.ds(2 * s, 2 * (e - s))
            for d in (1, 2, 3, 0):
                to = (p, 4 * yy + (x + d) % 4)

                def go():
                    send(e_ref.at[rows], h.at[rows, col], ysend, yrecv.at[i], to)

                if d:
                    go()
                else:
                    pl.when(y != yy)(go)

    def peer(d):
        return (2 * ((z + d) % 8) + 1, col)

    @pl.when(has_b)
    def _():
        send(b_hbm, ball.at[p], bsend, brecv.at[p], peer(1))
        send(b_hbm, ball.at[p], bsend, brecv.at[p], peer(7))

        @pl.when(jnp.logical_not(solver))
        def _():
            send(b_hbm, ball.at[p], bsend, brecv.at[p], peer(0))

    def tiles(s):
        return (z + s) % 8

    def await_tile(t):
        both(ball.at[t], brecv.at[t]).wait()

    def hand_on(s, d):
        src = tiles(s)

        @pl.when(jnp.logical_and(solver, src < 2 * y))
        def _():
            for k in range(2):
                t = 2 * src + k
                await_tile(t)
                send(ball.at[t], ball.at[t], bsend, brecv.at[t], peer(d))

    hand_on(-1, 1)
    hand_on(1, -1)

    @pl.when(solver)
    def _():
        load_g.wait()
        for t in range(4):
            g = gbuf[:, 256 * t : 256 * t + 256]
            hi = g.astype(BF16)
            ghl[t, :256] = hi
            ghl[t, 256:] = (g - hi.astype(F32)).astype(BF16)

    own_y.wait()
    acc = jnp.zeros((32, 256), F32)
    for i, (s, e) in enumerate(zip(SPLIT, SPLIT[1:])):
        loads[i].wait()
        both(h.at[pl.ds(2 * s, 2 * (e - s)), pl.ds(0, 15)], yrecv.at[i]).wait()
        for t in range(s, e):
            lhs = jnp.concatenate([h[2 * t].reshape(32, 128), h[2 * t + 1].reshape(32, 128)], axis=1)
            acc += jnp.dot(lhs, abuf[t], preferred_element_type=F32)
    part[...] = acc.reshape(8, 4, 256)

    for d in (4, 3, 5, 2, 6, 1, 7):
        to = (z + d) % 8
        send(part.at[to], pin.at[p], psem.at[0], psem.at[1], (2 * to + 1, col))

    @pl.when(jnp.logical_not(solver))
    def _():
        send(part.at[z], pin.at[p], psem.at[0], psem.at[1], (p + 1, col))

    hand_on(-2, 1)
    hand_on(2, -1)
    hand_on(-3, 1)

    @pl.when(solver)
    def _():
        pin[p] = part[z]
        for s in (3, 4):

            @pl.when(tiles(s) < 2 * y)
            def _():
                await_tile(2 * tiles(s))
                await_tile(2 * tiles(s) + 1)

        @pl.when(has_b)
        def _():
            await_tile(p - 1)
            own_b.wait()

        load_r.wait()
        both(pin.at[pl.ds(0, 15)], psem.at[1]).wait()
        upd[...] = r_ref[...].reshape(4, 256) - jnp.sum(pin[...], axis=0)

        for i in range(3):

            @pl.when(y > i)
            def _():
                both(xin.at[i], xrecv.at[i]).wait()
                solved = jnp.sum(xin[i], axis=0).astype(BF16)
                total = jnp.dot(solved[0], ball[4 * i], preferred_element_type=F32)
                for k in range(1, 4):
                    total += jnp.dot(solved[k], ball[4 * i + k], preferred_element_type=F32)
                upd[...] -= total

        remain = upd[...]
        low = remain - remain.astype(BF16).astype(F32)
        lhs = jnp.concatenate([remain, low], axis=0).astype(BF16)
        lhs = jnp.concatenate([lhs, lhs], axis=1)
        for t in range(4):
            res = jnp.dot(lhs, ghl[t], preferred_element_type=F32)
            gp[t] = res[:4] + res[4:]

        for j in range(1, 4):

            @pl.when(y < j)
            def _():
                for d in (2, 1, 3, 0):
                    send(gp, xin.at[y, x], xsend.at[j], xrecv.at[y], (p, 4 * j + (x + d) % 4))

        for d in (2, 1, 3):
            to = (x + d) % 4
            send(gp.at[to], oin.at[x], osem.at[0], osem.at[1], (p, 4 * y + to))
        oin[x] = gp[x]
        both(oin.at[pl.ds(0, 3)], osem.at[1]).wait()
        total = jnp.sum(oin[...], axis=0).reshape(4, 1, 256)
        ob[...] = total
        for d in (4, 3, 5, 2, 6, 1, 7):
            for k in range(2):
                send(ob, o_ref.at[z], fsem.at[0], fsem.at[1], (2 * ((z + d) % 8) + k, col))
        send(ob, o_ref.at[z], fsem.at[0], fsem.at[1], (p - 1, col))
        o_ref[z] = total
        both(o_ref.at[pl.ds(0, 7)], fsem.at[1]).wait()

        for j in range(1, 4):

            @pl.when(y < j)
            def _():
                both(xin.at[0], xsend.at[j]).wait()

        both(oin.at[pl.ds(0, 3)], osem.at[0]).wait()
        both(pin.at[pl.ds(0, 7)], psem.at[0]).wait()
        both(pin.at[pl.ds(0, 15)], fsem.at[0]).wait()
        for s in (-1, 1, -2, 2, -3):

            @pl.when(tiles(s) < 2 * y)
            def _():
                both(ball.at[pl.ds(0, 2)], bsend).wait()

        @pl.when(has_b)
        def _():
            both(ball.at[pl.ds(0, 2)], bsend).wait()

    @pl.when(jnp.logical_not(solver))
    def _():
        both(pin.at[pl.ds(0, 8)], psem.at[0]).wait()

        @pl.when(has_b)
        def _():
            both(ball.at[pl.ds(0, 3)], bsend).wait()

        both(o_ref, fsem.at[1]).wait()

    both(h.at[:, pl.ds(0, 15)], ysend).wait()


def local(panel_pre, tail_panel, earlier, right_side, inverses):
    turns = panel_pre.shape[0]
    a = panel_pre.reshape(turns, 256, 256)
    b = tail_panel.reshape(256, 256)
    e = earlier.reshape(2, turns, 2, 128).transpose(1, 2, 0, 3).reshape(2 * turns, 2, 128)
    r = right_side.reshape(8, 4, 1, 256)
    g = inverses.reshape(256, 1024)
    dma = pltpu.SemaphoreType.DMA
    out = pl.pallas_call(
        kernel,
        out_shape=jax.ShapeDtypeStruct((8, 4, 1, 256), F32),
        in_specs=[pl.BlockSpec(memory_space=pltpu.HBM)] * 5,
        out_specs=pl.BlockSpec(memory_space=pltpu.VMEM),
        scratch_shapes=[
            pltpu.VMEM((2 * turns, 2, 128), BF16),
            pltpu.VMEM((4, 1, 256), F32),
            pltpu.VMEM((turns, 256, 256), BF16),
            pltpu.VMEM((12, 256, 256), BF16),
            pltpu.VMEM((256, 1024), F32),
            pltpu.VMEM((4, 512, 256), BF16),
            pltpu.VMEM((2 * turns, 16, 2, 128), BF16),
            pltpu.VMEM((8, 4, 256), F32),
            pltpu.VMEM((16, 4, 256), F32),
            pltpu.VMEM((4, 256), F32),
            pltpu.VMEM((4, 4, 256), F32),
            pltpu.VMEM((3, 4, 4, 4, 256), F32),
            pltpu.VMEM((4, 4, 256), F32),
            pltpu.VMEM((4, 1, 256), F32),
            dma((7,)),
            dma,
            dma((2,)),
            dma,
            dma((12,)),
            dma((2,)),
            dma((4,)),
            dma((3,)),
            dma((2,)),
            dma((2,)),
        ],
        compiler_params=pltpu.CompilerParams(collective_id=0, has_side_effects=True, vmem_limit_bytes=64 << 20),
        cost_estimate=pl.CostEstimate(flops=2 * 32 * 256 * 256 * turns, bytes_accessed=6 << 20, transcendentals=0),
        name="solve",
    )(a, b, e, r, g)
    return out.reshape(32, 1, 1, 256)


def solution(mesh):
    in_specs = (
        P(None, "prow", None, None, "pcol", None),
        P(None, "prow", None, None, "pcol", None),
        P("pcol", None, "prow", None),
        P(None, None, "pcol", None),
        P(None, "pcol", None, None),
    )
    out_specs = P(None, None, "pcol", None)
    return jax.shard_map(local, mesh=mesh, in_specs=in_specs, out_specs=out_specs, check_vma=False)
```

```python
import jax
import jax.numpy as jnp
from jax import lax
from jax.experimental import pallas as pl
from jax.experimental.pallas import tpu as pltpu
from jax.sharding import PartitionSpec as P

MESH = pl.DeviceIdType.MESH
F32 = jnp.float32
BF16 = jnp.bfloat16
SPLIT = (0, 16, 31)
LEVEL = (4, 5, 6, 7, 1, 0, 2, 3)


def kernel(a_hbm, b_hbm, e_hbm, r_hbm, g_hbm, o_ref, e_ref, r_ref, abuf, ball, gbuf, ghl, h, part, pin, upd, gp, xin, oin, ob, lsem, ysend, yrecv, bsend, brecv, psem, xsend, xrecv, osem, fsem):
    p = lax.axis_index("prow")
    col = lax.axis_index("pcol")
    z, core = p // 2, p % 2
    y, x = col // 4, col % 4
    solver = core == 1
    group = sum(jnp.where(z == level, k, 0) for k, level in enumerate(LEVEL))

    def both(ref, sem):
        return pltpu.make_async_copy(ref, ref, sem)

    def send(src, dst, ssem, rsem, to):
        pltpu.make_async_remote_copy(src, dst, ssem, rsem, device_id=to, device_id_type=MESH).start()

    load_y = pltpu.make_async_copy(e_hbm, e_ref, lsem.at[0])
    own_y = pltpu.make_async_copy(e_hbm, h.at[:, col], lsem.at[1])
    load_r = pltpu.make_async_copy(r_hbm.at[group], r_ref, lsem.at[2])
    load_g = pltpu.make_async_copy(g_hbm, gbuf, lsem.at[3])
    own_b = pltpu.make_async_copy(b_hbm, ball.at[p], lsem.at[4])
    chunks = [pl.ds(s, e - s) for s, e in zip(SPLIT, SPLIT[1:])]
    loads = [pltpu.make_async_copy(a_hbm.at[c], abuf.at[c], lsem.at[5 + i]) for i, c in enumerate(chunks)]
    has_b = p < 4 * y

    load_y.start()
    own_y.start()
    loads[0].start()

    @pl.when(solver)
    def _():
        load_g.start()
        load_r.start()

        @pl.when(has_b)
        def _():
            own_b.start()

    loads[1].start()

    barrier = pltpu.get_barrier_semaphore()
    for d in range(1, 16):
        pl.semaphore_signal(barrier, inc=1, device_id=(p, (col + d) % 16), device_id_type=MESH)
        pl.semaphore_signal(barrier, inc=1, device_id=((p + d) % 16, col), device_id_type=MESH)
    load_y.wait()
    pl.semaphore_wait(barrier, 30)

    for yy in range(4):
        for i, (s, e) in enumerate(zip(SPLIT, SPLIT[1:])):
            rows = pl.ds(2 * s, 2 * (e - s))
            for d in (1, 2, 3, 0):
                to = (p, 4 * yy + (x + d) % 4)

                def go():
                    send(e_ref.at[rows], h.at[rows, col], ysend, yrecv.at[y // 2 * 2 + i], to)

                if d:
                    go()
                else:
                    pl.when(y != yy)(go)

    def peer(d):
        return (2 * ((z + d) % 8) + 1, col)

    @pl.when(has_b)
    def _():
        send(b_hbm, ball.at[p], bsend, brecv.at[p], peer(1))
        send(b_hbm, ball.at[p], bsend, brecv.at[p], peer(7))

        @pl.when(jnp.logical_not(solver))
        def _():
            send(b_hbm, ball.at[p], bsend, brecv.at[p], peer(0))

    def tiles(s):
        return (z + s) % 8

    def await_tile(t):
        both(ball.at[t], brecv.at[t]).wait()

    def hand_on(s, d):
        src = tiles(s)

        @pl.when(jnp.logical_and(solver, src < 2 * y))
        def _():
            for k in range(2):
                t = 2 * src + k
                await_tile(t)
                send(ball.at[t], ball.at[t], bsend, brecv.at[t], peer(d))

    hand_on(-1, 1)
    hand_on(1, -1)

    @pl.when(solver)
    def _():
        load_g.wait()
        for t in range(4):
            g = gbuf[:, 256 * t : 256 * t + 256]
            hi = g.astype(BF16)
            ghl[t, :256] = hi
            ghl[t, 256:] = (g - hi.astype(F32)).astype(BF16)

    own_y.wait()
    for half in range(2):
        acc = jnp.zeros((16, 256), F32)
        for i, (s, e) in enumerate(zip(SPLIT, SPLIT[1:])):
            if half == 0:
                loads[i].wait()
            rows, got = pl.ds(2 * s, 2 * (e - s)), yrecv.at[2 * half + i]

            @pl.when(y // 2 == half)
            def _():
                both(h.at[rows, pl.ds(0, 7)], got).wait()

            @pl.when(y // 2 != half)
            def _():
                both(h.at[rows, pl.ds(0, 8)], got).wait()

            for t in range(s, e):
                lhs = jnp.concatenate([h[2 * t + k, 8 * half : 8 * half + 8].reshape(16, 128) for k in range(2)], axis=1)
                acc += jnp.dot(lhs, abuf[t], preferred_element_type=F32)
        part[4 * half : 4 * half + 4] = acc.reshape(4, 4, 256)

        for k in range(4 * half, 4 * half + 4):
            to = 2 * LEVEL[k] + 1

            @pl.when(p != to)
            def _():
                send(part.at[k], pin.at[p], psem.at[0], psem.at[1], (to, col))

        if half == 0:
            hand_on(-2, 1)
            hand_on(2, -1)

    hand_on(-3, 1)

    @pl.when(solver)
    def _():
        pin[p] = part[group]
        for s in (3, 4):

            @pl.when(tiles(s) < 2 * y)
            def _():
                await_tile(2 * tiles(s))
                await_tile(2 * tiles(s) + 1)

        @pl.when(has_b)
        def _():
            await_tile(p - 1)
            own_b.wait()

        load_r.wait()
        both(pin.at[pl.ds(0, 15)], psem.at[1]).wait()
        upd[...] = r_ref[...].reshape(4, 256) - jnp.sum(pin[...], axis=0)

        for i in range(3):

            @pl.when(y > i)
            def _():
                both(xin.at[i], xrecv.at[i]).wait()
                solved = jnp.sum(xin[i], axis=0).astype(BF16)
                total = jnp.dot(solved[0], ball[4 * i], preferred_element_type=F32)
                for k in range(1, 4):
                    total += jnp.dot(solved[k], ball[4 * i + k], preferred_element_type=F32)
                upd[...] -= total

        remain = upd[...]
        low = remain - remain.astype(BF16).astype(F32)
        lhs = jnp.concatenate([remain, low], axis=0).astype(BF16)
        lhs = jnp.concatenate([lhs, lhs], axis=1)
        for t in range(4):
            res = jnp.dot(lhs, ghl[t], preferred_element_type=F32)
            gp[t] = res[:4] + res[4:]

        for j in range(1, 4):

            @pl.when(y < j)
            def _():
                for d in (2, 1, 3, 0):
                    send(gp, xin.at[y, x], xsend.at[j], xrecv.at[y], (p, 4 * j + (x + d) % 4))

        for d in (2, 1, 3):
            to = (x + d) % 4
            send(gp.at[to], oin.at[x], osem.at[0], osem.at[1], (p, 4 * y + to))
        oin[x] = gp[x]
        both(oin.at[pl.ds(0, 3)], osem.at[1]).wait()
        total = jnp.sum(oin[...], axis=0).reshape(4, 1, 256)
        ob[...] = total
        for to in (1, 0, 3, 2, 5, 4, 7, 6, 15, 14, 9, 8, 13, 12, 11, 10):

            @pl.when(p != to)
            def _():
                send(ob, o_ref.at[group], fsem.at[0], fsem.at[1], (to, col))

        o_ref[group] = total
        both(o_ref.at[pl.ds(0, 7)], fsem.at[1]).wait()

        for j in range(1, 4):

            @pl.when(y < j)
            def _():
                both(xin.at[0], xsend.at[j]).wait()

        both(oin.at[pl.ds(0, 3)], osem.at[0]).wait()
        both(pin.at[pl.ds(0, 7)], psem.at[0]).wait()
        both(pin.at[pl.ds(0, 15)], fsem.at[0]).wait()
        for s in (-1, 1, -2, 2, -3):

            @pl.when(tiles(s) < 2 * y)
            def _():
                both(ball.at[pl.ds(0, 2)], bsend).wait()

        @pl.when(has_b)
        def _():
            both(ball.at[pl.ds(0, 2)], bsend).wait()

    @pl.when(jnp.logical_not(solver))
    def _():
        both(pin.at[pl.ds(0, 8)], psem.at[0]).wait()

        @pl.when(has_b)
        def _():
            both(ball.at[pl.ds(0, 3)], bsend).wait()

        both(o_ref, fsem.at[1]).wait()

    both(h.at[:, pl.ds(0, 15)], ysend).wait()


def local(panel_pre, tail_panel, earlier, right_side, inverses):
    turns = panel_pre.shape[0]
    a = panel_pre.reshape(turns, 256, 256)
    b = tail_panel.reshape(256, 256)
    e = earlier.reshape(2, turns, 2, 128).transpose(1, 2, 0, 3).reshape(2 * turns, 2, 128)
    r = right_side.reshape(8, 4, 1, 256)
    g = inverses.reshape(256, 1024)
    dma = pltpu.SemaphoreType.DMA
    out = pl.pallas_call(
        kernel,
        out_shape=jax.ShapeDtypeStruct((8, 4, 1, 256), F32),
        in_specs=[pl.BlockSpec(memory_space=pltpu.HBM)] * 5,
        out_specs=pl.BlockSpec(memory_space=pltpu.VMEM),
        scratch_shapes=[
            pltpu.VMEM((2 * turns, 2, 128), BF16),
            pltpu.VMEM((4, 1, 256), F32),
            pltpu.VMEM((turns, 256, 256), BF16),
            pltpu.VMEM((12, 256, 256), BF16),
            pltpu.VMEM((256, 1024), F32),
            pltpu.VMEM((4, 512, 256), BF16),
            pltpu.VMEM((2 * turns, 16, 2, 128), BF16),
            pltpu.VMEM((8, 4, 256), F32),
            pltpu.VMEM((16, 4, 256), F32),
            pltpu.VMEM((4, 256), F32),
            pltpu.VMEM((4, 4, 256), F32),
            pltpu.VMEM((3, 4, 4, 4, 256), F32),
            pltpu.VMEM((4, 4, 256), F32),
            pltpu.VMEM((4, 1, 256), F32),
            dma((7,)),
            dma,
            dma((4,)),
            dma,
            dma((12,)),
            dma((2,)),
            dma((4,)),
            dma((3,)),
            dma((2,)),
            dma((2,)),
        ],
        compiler_params=pltpu.CompilerParams(collective_id=0, has_side_effects=True, vmem_limit_bytes=64 << 20),
        cost_estimate=pl.CostEstimate(flops=2 * 32 * 256 * 256 * turns, bytes_accessed=6 << 20, transcendentals=0),
        name="solve",
    )(a, b, e, r, g)
    return out.reshape(32, 1, 1, 256)


def solution(mesh):
    in_specs = (
        P(None, "prow", None, None, "pcol", None),
        P(None, "prow", None, None, "pcol", None),
        P("pcol", None, "prow", None),
        P(None, None, "pcol", None),
        P(None, "pcol", None, None),
    )
    out_specs = P(None, None, "pcol", None)
    return jax.shard_map(local, mesh=mesh, in_specs=in_specs, out_specs=out_specs, check_vma=False)
```

```python
import jax
import jax.numpy as jnp
from jax import lax
from jax.experimental import pallas as pl
from jax.experimental.pallas import tpu as pltpu
from jax.sharding import PartitionSpec as P

MESH = pl.DeviceIdType.MESH
F32 = jnp.float32
BF16 = jnp.bfloat16
SPLIT = (0, 16, 31)
LEVEL = (4, 5, 6, 7, 1, 0, 2, 3)


def kernel(a_hbm, b_hbm, e_hbm, r_hbm, g_hbm, o_ref, e_ref, r_ref, abuf, ball, gbuf, ghl, h, part, pin, upd, gp, xin, oin, ob, lsem, ysend, yrecv, bsend, brecv, psem, xsend, xrecv, osem, fsem, tok):
    p = lax.axis_index("prow")
    col = lax.axis_index("pcol")
    z, core = p // 2, p % 2
    y, x = col // 4, col % 4
    solver = core == 1
    group = sum(jnp.where(z == level, k, 0) for k, level in enumerate(LEVEL))

    def both(ref, sem):
        return pltpu.make_async_copy(ref, ref, sem)

    def send(src, dst, ssem, rsem, to):
        pltpu.make_async_remote_copy(src, dst, ssem, rsem, device_id=to, device_id_type=MESH).start()

    load_y = pltpu.make_async_copy(e_hbm, e_ref, lsem.at[0])
    own_y = pltpu.make_async_copy(e_hbm, h.at[:, col], lsem.at[1])
    load_r = pltpu.make_async_copy(r_hbm.at[group], r_ref, lsem.at[2])
    load_g = pltpu.make_async_copy(g_hbm, gbuf, lsem.at[3])
    own_b = pltpu.make_async_copy(b_hbm, ball.at[p], lsem.at[4])
    chunks = [pl.ds(s, e - s) for s, e in zip(SPLIT, SPLIT[1:])]
    loads = [pltpu.make_async_copy(a_hbm.at[c], abuf.at[c], lsem.at[5 + i]) for i, c in enumerate(chunks)]
    has_b = p < 4 * y

    load_y.start()
    own_y.start()
    loads[0].start()

    @pl.when(solver)
    def _():
        load_g.start()
        load_r.start()

        @pl.when(has_b)
        def _():
            own_b.start()

    loads[1].start()

    def peer(d):
        return (2 * ((z + d) % 8) + 1, col)

    def signal(sem, to):
        pl.semaphore_signal(sem, inc=1, device_id=to, device_id_type=MESH)

    barrier = pltpu.get_barrier_semaphore()
    for dy in (2, 1, 3, 0):
        for dx in (2, 1, 3, 0):
            if dy or dx:
                signal(barrier, (p, (y + dy) % 4 * 4 + (x + dx) % 4))

    signal(barrier, (p + 1 - 2 * core, col))

    @pl.when(core == 1)
    def _():
        for d in (1, 7):
            for k in range(2):
                signal(barrier, (2 * ((z + d) % 8) + k, col))

    load_y.wait()
    pl.semaphore_wait(barrier, 18)

    def hear(up, down):
        @pl.when(core == 1)
        def _():
            pl.semaphore_wait(tok.at[0], 1)
            if up:
                signal(tok.at[0], peer(1))
            if down is not None:
                pl.semaphore_wait(tok.at[1], 1)
            if down:
                signal(tok.at[1], peer(7))

    @pl.when(core == 1)
    def _():
        signal(tok.at[0], peer(1))
        signal(tok.at[1], peer(7))

    for yy in range(4):
        for i, (s, e) in enumerate(zip(SPLIT, SPLIT[1:])):
            rows = pl.ds(2 * s, 2 * (e - s))
            for d in (1, 2, 3, 0):
                to = (p, 4 * yy + (x + d) % 4)

                def go():
                    send(e_ref.at[rows], h.at[rows, col], ysend, yrecv.at[y // 2 * 2 + i], to)

                if d:
                    go()
                else:
                    pl.when(y != yy)(go)

    @pl.when(has_b)
    def _():
        send(b_hbm, ball.at[p], bsend, brecv.at[p], peer(1))
        send(b_hbm, ball.at[p], bsend, brecv.at[p], peer(7))

        @pl.when(jnp.logical_not(solver))
        def _():
            send(b_hbm, ball.at[p], bsend, brecv.at[p], peer(0))

    def tiles(s):
        return (z + s) % 8

    def await_tile(t):
        both(ball.at[t], brecv.at[t]).wait()

    def hand_on(s, d):
        src = tiles(s)

        @pl.when(jnp.logical_and(solver, src < 2 * y))
        def _():
            for k in range(2):
                t = 2 * src + k
                await_tile(t)
                send(ball.at[t], ball.at[t], bsend, brecv.at[t], peer(d))

    hear(True, True)
    hand_on(-1, 1)
    hand_on(1, -1)
    hear(True, False)

    @pl.when(solver)
    def _():
        load_g.wait()
        for t in range(4):
            g = gbuf[:, 256 * t : 256 * t + 256]
            hi = g.astype(BF16)
            ghl[t, :256] = hi
            ghl[t, 256:] = (g - hi.astype(F32)).astype(BF16)

    own_y.wait()
    hear(False, None)

    @pl.when(core == 1)
    def _():
        signal(tok.at[2], (p - 1, col))

    for half in range(2):
        acc = jnp.zeros((16, 256), F32)
        for i, (s, e) in enumerate(zip(SPLIT, SPLIT[1:])):
            if half == 0:
                loads[i].wait()
            rows, got = pl.ds(2 * s, 2 * (e - s)), yrecv.at[2 * half + i]

            @pl.when(y // 2 == half)
            def _():
                both(h.at[rows, pl.ds(0, 7)], got).wait()

            @pl.when(y // 2 != half)
            def _():
                both(h.at[rows, pl.ds(0, 8)], got).wait()

            for t in range(s, e):
                lhs = jnp.concatenate([h[2 * t + k, 8 * half : 8 * half + 8].reshape(16, 128) for k in range(2)], axis=1)
                acc += jnp.dot(lhs, abuf[t], preferred_element_type=F32)
        part[4 * half : 4 * half + 4] = acc.reshape(4, 4, 256)

        if half == 0:

            @pl.when(core == 0)
            def _():
                pl.semaphore_wait(tok.at[2], 1)

        for k in range(4 * half, 4 * half + 4):
            to = 2 * LEVEL[k] + 1

            @pl.when(p != to)
            def _():
                send(part.at[k], pin.at[p], psem.at[0], psem.at[1], (to, col))

        if half == 0:
            hand_on(-2, 1)
            hand_on(2, -1)

    hand_on(-3, 1)

    @pl.when(solver)
    def _():
        pin[p] = part[group]
        for s in (3, 4):

            @pl.when(tiles(s) < 2 * y)
            def _():
                await_tile(2 * tiles(s))
                await_tile(2 * tiles(s) + 1)

        @pl.when(has_b)
        def _():
            await_tile(p - 1)
            own_b.wait()

        load_r.wait()
        both(pin.at[pl.ds(0, 15)], psem.at[1]).wait()
        upd[...] = r_ref[...].reshape(4, 256) - jnp.sum(pin[...], axis=0)

        for i in range(3):

            @pl.when(y > i)
            def _():
                both(xin.at[i], xrecv.at[i]).wait()
                solved = jnp.sum(xin[i], axis=0).astype(BF16)
                total = jnp.dot(solved[0], ball[4 * i], preferred_element_type=F32)
                for k in range(1, 4):
                    total += jnp.dot(solved[k], ball[4 * i + k], preferred_element_type=F32)
                upd[...] -= total

        remain = upd[...]
        low = remain - remain.astype(BF16).astype(F32)
        lhs = jnp.concatenate([remain, low], axis=0).astype(BF16)
        lhs = jnp.concatenate([lhs, lhs], axis=1)
        for t in range(4):
            res = jnp.dot(lhs, ghl[t], preferred_element_type=F32)
            gp[t] = res[:4] + res[4:]

        for j in range(1, 4):

            @pl.when(y < j)
            def _():
                for d in (2, 1, 3, 0):
                    send(gp, xin.at[y, x], xsend.at[j], xrecv.at[y], (p, 4 * j + (x + d) % 4))

        for d in (2, 1, 3):
            to = (x + d) % 4
            send(gp.at[to], oin.at[x], osem.at[0], osem.at[1], (p, 4 * y + to))
        oin[x] = gp[x]
        both(oin.at[pl.ds(0, 3)], osem.at[1]).wait()
        total = jnp.sum(oin[...], axis=0).reshape(4, 1, 256)
        ob[...] = total
        for to in (1, 0, 3, 2, 5, 4, 7, 6, 15, 14, 9, 8, 13, 12, 11, 10):

            @pl.when(p != to)
            def _():
                send(ob, o_ref.at[group], fsem.at[0], fsem.at[1], (to, col))

        o_ref[group] = total
        both(o_ref.at[pl.ds(0, 7)], fsem.at[1]).wait()

        for j in range(1, 4):

            @pl.when(y < j)
            def _():
                both(xin.at[0], xsend.at[j]).wait()

        both(oin.at[pl.ds(0, 3)], osem.at[0]).wait()
        both(pin.at[pl.ds(0, 7)], psem.at[0]).wait()
        both(pin.at[pl.ds(0, 15)], fsem.at[0]).wait()
        for s in (-1, 1, -2, 2, -3):

            @pl.when(tiles(s) < 2 * y)
            def _():
                both(ball.at[pl.ds(0, 2)], bsend).wait()

        @pl.when(has_b)
        def _():
            both(ball.at[pl.ds(0, 2)], bsend).wait()

    @pl.when(jnp.logical_not(solver))
    def _():
        both(pin.at[pl.ds(0, 8)], psem.at[0]).wait()

        @pl.when(has_b)
        def _():
            both(ball.at[pl.ds(0, 3)], bsend).wait()

        both(o_ref, fsem.at[1]).wait()

    both(h.at[:, pl.ds(0, 15)], ysend).wait()


def local(panel_pre, tail_panel, earlier, right_side, inverses):
    turns = panel_pre.shape[0]
    a = panel_pre.reshape(turns, 256, 256)
    b = tail_panel.reshape(256, 256)
    e = earlier.reshape(2, turns, 2, 128).transpose(1, 2, 0, 3).reshape(2 * turns, 2, 128)
    r = right_side.reshape(8, 4, 1, 256)
    g = inverses.reshape(256, 1024)
    dma = pltpu.SemaphoreType.DMA
    out = pl.pallas_call(
        kernel,
        out_shape=jax.ShapeDtypeStruct((8, 4, 1, 256), F32),
        in_specs=[pl.BlockSpec(memory_space=pltpu.HBM)] * 5,
        out_specs=pl.BlockSpec(memory_space=pltpu.VMEM),
        scratch_shapes=[
            pltpu.VMEM((2 * turns, 2, 128), BF16),
            pltpu.VMEM((4, 1, 256), F32),
            pltpu.VMEM((turns, 256, 256), BF16),
            pltpu.VMEM((12, 256, 256), BF16),
            pltpu.VMEM((256, 1024), F32),
            pltpu.VMEM((4, 512, 256), BF16),
            pltpu.VMEM((2 * turns, 16, 2, 128), BF16),
            pltpu.VMEM((8, 4, 256), F32),
            pltpu.VMEM((16, 4, 256), F32),
            pltpu.VMEM((4, 256), F32),
            pltpu.VMEM((4, 4, 256), F32),
            pltpu.VMEM((3, 4, 4, 4, 256), F32),
            pltpu.VMEM((4, 4, 256), F32),
            pltpu.VMEM((4, 1, 256), F32),
            dma((7,)),
            dma,
            dma((4,)),
            dma,
            dma((12,)),
            dma((2,)),
            dma((4,)),
            dma((3,)),
            dma((2,)),
            dma((2,)),
            pltpu.SemaphoreType.REGULAR((3,)),
        ],
        compiler_params=pltpu.CompilerParams(collective_id=0, has_side_effects=True, vmem_limit_bytes=64 << 20),
        cost_estimate=pl.CostEstimate(flops=2 * 32 * 256 * 256 * turns, bytes_accessed=6 << 20, transcendentals=0),
        name="solve",
    )(a, b, e, r, g)
    return out.reshape(32, 1, 1, 256)


def solution(mesh):
    in_specs = (
        P(None, "prow", None, None, "pcol", None),
        P(None, "prow", None, None, "pcol", None),
        P("pcol", None, "prow", None),
        P(None, None, "pcol", None),
        P(None, "pcol", None, None),
    )
    out_specs = P(None, None, "pcol", None)
    return jax.shard_map(local, mesh=mesh, in_specs=in_specs, out_specs=out_specs, check_vma=False)
```

```python
import jax
import jax.numpy as jnp
from jax import lax
from jax.experimental import pallas as pl
from jax.experimental.pallas import tpu as pltpu
from jax.sharding import PartitionSpec as P

MESH = pl.DeviceIdType.MESH
F32 = jnp.float32
BF16 = jnp.bfloat16
SPLIT = (0, 16, 31)
LEVEL = (4, 3, 5, 2, 0, 7, 6, 1)


def kernel(a_hbm, b_hbm, e_hbm, r_hbm, g_hbm, o_ref, e_ref, r_ref, abuf, ball, gbuf, ghl, h, part, pin, upd, gp, xin, oin, ob, lsem, ysend, yrecv, bsend, brecv, psem, xsend, xrecv, osem, fsem, tok):
    p = lax.axis_index("prow")
    col = lax.axis_index("pcol")
    z, core = p // 2, p % 2
    y, x = col // 4, col % 4
    solver = core == 1
    group = sum(jnp.where(z == level, k, 0) for k, level in enumerate(LEVEL))

    def both(ref, sem):
        return pltpu.make_async_copy(ref, ref, sem)

    def send(src, dst, ssem, rsem, to):
        pltpu.make_async_remote_copy(src, dst, ssem, rsem, device_id=to, device_id_type=MESH).start()

    load_y = pltpu.make_async_copy(e_hbm, e_ref, lsem.at[0])
    own_y = pltpu.make_async_copy(e_hbm, h.at[:, col], lsem.at[1])
    load_r = pltpu.make_async_copy(r_hbm.at[group], r_ref, lsem.at[2])
    load_g = pltpu.make_async_copy(g_hbm, gbuf, lsem.at[3])
    own_b = pltpu.make_async_copy(b_hbm, ball.at[p], lsem.at[4])
    chunks = [pl.ds(s, e - s) for s, e in zip(SPLIT, SPLIT[1:])]
    loads = [pltpu.make_async_copy(a_hbm.at[c], abuf.at[c], lsem.at[5 + i]) for i, c in enumerate(chunks)]
    has_b = p < 4 * y

    load_y.start()
    own_y.start()
    loads[0].start()

    @pl.when(solver)
    def _():
        load_g.start()
        load_r.start()

        @pl.when(has_b)
        def _():
            own_b.start()

    loads[1].start()

    def peer(d):
        return (2 * ((z + d) % 8) + 1, col)

    def signal(sem, to):
        pl.semaphore_signal(sem, inc=1, device_id=to, device_id_type=MESH)

    barrier = pltpu.get_barrier_semaphore()
    for dy in (2, 1, 3, 0):
        for dx in (2, 1, 3, 0):
            if dy or dx:
                signal(barrier, (p, (y + dy) % 4 * 4 + (x + dx) % 4))

    signal(barrier, (p + 1 - 2 * core, col))

    @pl.when(core == 1)
    def _():
        for d in (1, 7):
            for k in range(2):
                signal(barrier, (2 * ((z + d) % 8) + k, col))

    load_y.wait()
    pl.semaphore_wait(barrier, 18)

    def hear(up, down):
        @pl.when(core == 1)
        def _():
            pl.semaphore_wait(tok.at[0], 1)
            if up:
                signal(tok.at[0], peer(1))
            if down is not None:
                pl.semaphore_wait(tok.at[1], 1)
            if down:
                signal(tok.at[1], peer(7))

    @pl.when(core == 1)
    def _():
        signal(tok.at[0], peer(1))
        signal(tok.at[1], peer(7))

    for yy in range(4):
        for i, (s, e) in enumerate(zip(SPLIT, SPLIT[1:])):
            rows = pl.ds(2 * s, 2 * (e - s))
            for d in (2, 1, 3, 0):
                to = (p, 4 * yy + (x + d) % 4)

                def go():
                    send(e_ref.at[rows], h.at[rows, col], ysend, yrecv.at[y // 2 * 2 + i], to)

                if d:
                    go()
                else:
                    pl.when(y != yy)(go)

    @pl.when(has_b)
    def _():
        send(b_hbm, ball.at[p], bsend, brecv.at[p], peer(1))
        send(b_hbm, ball.at[p], bsend, brecv.at[p], peer(7))

        @pl.when(jnp.logical_not(solver))
        def _():
            send(b_hbm, ball.at[p], bsend, brecv.at[p], peer(0))

    def tiles(s):
        return (z + s) % 8

    def await_tile(t):
        both(ball.at[t], brecv.at[t]).wait()

    def hand_on(s, d):
        src = tiles(s)

        @pl.when(jnp.logical_and(solver, src < 2 * y))
        def _():
            for k in range(2):
                t = 2 * src + k
                await_tile(t)
                send(ball.at[t], ball.at[t], bsend, brecv.at[t], peer(d))

    hear(True, True)
    hand_on(-1, 1)
    hand_on(1, -1)
    hear(True, False)

    @pl.when(solver)
    def _():
        load_g.wait()
        for t in range(4):
            g = gbuf[:, 256 * t : 256 * t + 256]
            hi = g.astype(BF16)
            ghl[t, :256] = hi
            ghl[t, 256:] = (g - hi.astype(F32)).astype(BF16)

    own_y.wait()
    hear(False, None)

    @pl.when(core == 1)
    def _():
        signal(tok.at[2], (p - 1, col))

    for half in range(2):
        acc = jnp.zeros((16, 256), F32)
        for i, (s, e) in enumerate(zip(SPLIT, SPLIT[1:])):
            if half == 0:
                loads[i].wait()
            rows, got = pl.ds(2 * s, 2 * (e - s)), yrecv.at[2 * half + i]

            @pl.when(y // 2 == half)
            def _():
                both(h.at[rows, pl.ds(0, 7)], got).wait()

            @pl.when(y // 2 != half)
            def _():
                both(h.at[rows, pl.ds(0, 8)], got).wait()

            for t in range(s, e):
                lhs = jnp.concatenate([h[2 * t + k, 8 * half : 8 * half + 8].reshape(16, 128) for k in range(2)], axis=1)
                acc += jnp.dot(lhs, abuf[t], preferred_element_type=F32)
        part[4 * half : 4 * half + 4] = acc.reshape(4, 4, 256)

        if half == 0:

            @pl.when(core == 0)
            def _():
                pl.semaphore_wait(tok.at[2], 1)

        for k in range(4 * half, 4 * half + 4):
            to = 2 * LEVEL[k] + 1

            @pl.when(p != to)
            def _():
                send(part.at[k], pin.at[p], psem.at[0], psem.at[1], (to, col))

        if half == 0:
            hand_on(-2, 1)
            hand_on(2, -1)

    hand_on(-3, 1)

    @pl.when(solver)
    def _():
        pin[p] = part[group]
        for s in (3, 4):

            @pl.when(tiles(s) < 2 * y)
            def _():
                await_tile(2 * tiles(s))
                await_tile(2 * tiles(s) + 1)

        @pl.when(has_b)
        def _():
            await_tile(p - 1)
            own_b.wait()

        load_r.wait()
        both(pin.at[pl.ds(0, 15)], psem.at[1]).wait()
        upd[...] = r_ref[...].reshape(4, 256) - jnp.sum(pin[...], axis=0)

        for i in range(3):

            @pl.when(y > i)
            def _():
                both(xin.at[i], xrecv.at[i]).wait()
                solved = jnp.sum(xin[i], axis=0).astype(BF16)
                total = jnp.dot(solved[0], ball[4 * i], preferred_element_type=F32)
                for k in range(1, 4):
                    total += jnp.dot(solved[k], ball[4 * i + k], preferred_element_type=F32)
                upd[...] -= total

        remain = upd[...]
        low = remain - remain.astype(BF16).astype(F32)
        lhs = jnp.concatenate([remain, low], axis=0).astype(BF16)
        lhs = jnp.concatenate([lhs, lhs], axis=1)
        for t in range(4):
            res = jnp.dot(lhs, ghl[t], preferred_element_type=F32)
            gp[t] = res[:4] + res[4:]

        for j in range(1, 4):

            @pl.when(y < j)
            def _():
                for d in (2, 1, 3, 0):
                    send(gp, xin.at[y, x], xsend.at[j], xrecv.at[y], (p, 4 * j + (x + d) % 4))

        for d in (2, 1, 3):
            to = (x + d) % 4
            send(gp.at[to], oin.at[x], osem.at[0], osem.at[1], (p, 4 * y + to))
        oin[x] = gp[x]
        both(oin.at[pl.ds(0, 3)], osem.at[1]).wait()
        total = jnp.sum(oin[...], axis=0).reshape(4, 1, 256)
        ob[...] = total
        for to in (1, 0, 3, 2, 5, 4, 7, 6, 15, 14, 9, 8, 13, 12, 11, 10):

            @pl.when(p != to)
            def _():
                send(ob, o_ref.at[group], fsem.at[0], fsem.at[1], (to, col))

        o_ref[group] = total
        both(o_ref.at[pl.ds(0, 7)], fsem.at[1]).wait()

        for j in range(1, 4):

            @pl.when(y < j)
            def _():
                both(xin.at[0], xsend.at[j]).wait()

        both(oin.at[pl.ds(0, 3)], osem.at[0]).wait()
        both(pin.at[pl.ds(0, 7)], psem.at[0]).wait()
        both(pin.at[pl.ds(0, 15)], fsem.at[0]).wait()
        for s in (-1, 1, -2, 2, -3):

            @pl.when(tiles(s) < 2 * y)
            def _():
                both(ball.at[pl.ds(0, 2)], bsend).wait()

        @pl.when(has_b)
        def _():
            both(ball.at[pl.ds(0, 2)], bsend).wait()

    @pl.when(jnp.logical_not(solver))
    def _():
        both(pin.at[pl.ds(0, 8)], psem.at[0]).wait()

        @pl.when(has_b)
        def _():
            both(ball.at[pl.ds(0, 3)], bsend).wait()

        both(o_ref, fsem.at[1]).wait()

    both(h.at[:, pl.ds(0, 15)], ysend).wait()


def local(panel_pre, tail_panel, earlier, right_side, inverses):
    turns = panel_pre.shape[0]
    a = panel_pre.reshape(turns, 256, 256)
    b = tail_panel.reshape(256, 256)
    e = earlier.reshape(2, turns, 2, 128).transpose(1, 2, 0, 3).reshape(2 * turns, 2, 128)
    r = right_side.reshape(8, 4, 1, 256)
    g = inverses.reshape(256, 1024)
    dma = pltpu.SemaphoreType.DMA
    out = pl.pallas_call(
        kernel,
        out_shape=jax.ShapeDtypeStruct((8, 4, 1, 256), F32),
        in_specs=[pl.BlockSpec(memory_space=pltpu.HBM)] * 5,
        out_specs=pl.BlockSpec(memory_space=pltpu.VMEM),
        scratch_shapes=[
            pltpu.VMEM((2 * turns, 2, 128), BF16),
            pltpu.VMEM((4, 1, 256), F32),
            pltpu.VMEM((turns, 256, 256), BF16),
            pltpu.VMEM((12, 256, 256), BF16),
            pltpu.VMEM((256, 1024), F32),
            pltpu.VMEM((4, 512, 256), BF16),
            pltpu.VMEM((2 * turns, 16, 2, 128), BF16),
            pltpu.VMEM((8, 4, 256), F32),
            pltpu.VMEM((16, 4, 256), F32),
            pltpu.VMEM((4, 256), F32),
            pltpu.VMEM((4, 4, 256), F32),
            pltpu.VMEM((3, 4, 4, 4, 256), F32),
            pltpu.VMEM((4, 4, 256), F32),
            pltpu.VMEM((4, 1, 256), F32),
            dma((7,)),
            dma,
            dma((4,)),
            dma,
            dma((12,)),
            dma((2,)),
            dma((4,)),
            dma((3,)),
            dma((2,)),
            dma((2,)),
            pltpu.SemaphoreType.REGULAR((3,)),
        ],
        compiler_params=pltpu.CompilerParams(collective_id=0, has_side_effects=True, vmem_limit_bytes=64 << 20),
        cost_estimate=pl.CostEstimate(flops=2 * 32 * 256 * 256 * turns, bytes_accessed=6 << 20, transcendentals=0),
        name="solve",
    )(a, b, e, r, g)
    return out.reshape(32, 1, 1, 256)


def solution(mesh):
    in_specs = (
        P(None, "prow", None, None, "pcol", None),
        P(None, "prow", None, None, "pcol", None),
        P("pcol", None, "prow", None),
        P(None, None, "pcol", None),
        P(None, "pcol", None, None),
    )
    out_specs = P(None, None, "pcol", None)
    return jax.shard_map(local, mesh=mesh, in_specs=in_specs, out_specs=out_specs, check_vma=False)
```

```python
import jax
import jax.numpy as jnp
from jax import lax
from jax.experimental import pallas as pl
from jax.experimental.pallas import tpu as pltpu
from jax.sharding import PartitionSpec as P

MESH = pl.DeviceIdType.MESH
F32 = jnp.float32
BF16 = jnp.bfloat16
SPLIT = (0, 16, 31)
LEVEL = (4, 3, 5, 2, 0, 7, 6, 1)


def kernel(a_hbm, b_hbm, e_hbm, r_hbm, g_hbm, o_ref, e_ref, r_ref, abuf, ball, gbuf, ghl, h, part, pin, upd, gp, xin, oin, ob, lsem, ysend, yrecv, bsend, brecv, psem, xsend, xrecv, osem, fsem, tok):
    p = lax.axis_index("prow")
    col = lax.axis_index("pcol")
    z, core = p // 2, p % 2
    y, x = col // 4, col % 4
    solver = core == 1
    group = sum(jnp.where(z == level, k, 0) for k, level in enumerate(LEVEL))

    def both(ref, sem):
        return pltpu.make_async_copy(ref, ref, sem)

    def send(src, dst, ssem, rsem, to):
        pltpu.make_async_remote_copy(src, dst, ssem, rsem, device_id=to, device_id_type=MESH).start()

    load_y = pltpu.make_async_copy(e_hbm, e_ref, lsem.at[0])
    own_y = pltpu.make_async_copy(e_hbm, h.at[:, col], lsem.at[1])
    load_r = pltpu.make_async_copy(r_hbm.at[group], r_ref, lsem.at[2])
    load_g = pltpu.make_async_copy(g_hbm, gbuf, lsem.at[3])
    own_b = pltpu.make_async_copy(b_hbm, ball.at[p], lsem.at[4])
    chunks = [pl.ds(s, e - s) for s, e in zip(SPLIT, SPLIT[1:])]
    loads = [pltpu.make_async_copy(a_hbm.at[c], abuf.at[c], lsem.at[5 + i]) for i, c in enumerate(chunks)]
    has_b = p < 4 * y

    load_y.start()
    own_y.start()
    loads[0].start()

    @pl.when(solver)
    def _():
        load_g.start()
        load_r.start()

        @pl.when(has_b)
        def _():
            own_b.start()

    loads[1].start()

    def peer(d):
        return (2 * ((z + d) % 8) + 1, col)

    def signal(sem, to):
        pl.semaphore_signal(sem, inc=1, device_id=to, device_id_type=MESH)

    barrier = pltpu.get_barrier_semaphore()
    for dy in (2, 1, 3, 0):
        for dx in (2, 1, 3, 0):
            if dy or dx:
                signal(barrier, (p, (y + dy) % 4 * 4 + (x + dx) % 4))

    signal(barrier, (p + 1 - 2 * core, col))

    for d, start in ((1, 7), (7, 4)):

        @pl.when(jnp.logical_and(core == 1, z != start))
        def _():
            for k in range(2):
                signal(barrier, (2 * ((z + d) % 8) + k, col))

    load_y.wait()
    edge = jnp.logical_or(z == 0, z == 3)
    pl.semaphore_wait(barrier, jnp.where(edge, 17, 18))

    def hear(up, down):
        @pl.when(core == 1)
        def _():
            pl.semaphore_wait(tok.at[0], 1)
            if up:
                signal(tok.at[0], peer(1))
            if down is not None:
                pl.semaphore_wait(tok.at[1], 1)
            if down:
                signal(tok.at[1], peer(7))

    def first_word():
        signal(tok.at[0], peer(1))
        signal(tok.at[1], peer(7))

    for d, start in ((1, 7), (7, 4)):

        @pl.when(jnp.logical_and(core == 1, z == start))
        def _():
            signal(tok.at[3], peer(d))

    @pl.when(jnp.logical_and(core == 1, jnp.logical_not(edge)))
    def _():
        first_word()

    for yy in range(4):
        for i, (s, e) in enumerate(zip(SPLIT, SPLIT[1:])):
            rows = pl.ds(2 * s, 2 * (e - s))
            for d in (2, 1, 3, 0):
                to = (p, 4 * yy + (x + d) % 4)

                def go():
                    send(e_ref.at[rows], h.at[rows, col], ysend, yrecv.at[y // 2 * 2 + i], to)

                if d:
                    go()
                else:
                    pl.when(y != yy)(go)

    def spread(d, when):
        @pl.when(jnp.logical_and(has_b, when))
        def _():
            send(b_hbm, ball.at[p], bsend, brecv.at[p], peer(d))

    spread(1, z != 3)
    spread(7, z != 0)
    spread(0, core == 0)

    @pl.when(jnp.logical_and(core == 1, edge))
    def _():
        pl.semaphore_wait(tok.at[3], 1)
        signal(tok.at[3], (p - 1, col))
        first_word()

    @pl.when(jnp.logical_and(core == 0, edge))
    def _():
        pl.semaphore_wait(tok.at[3], 1)

    spread(1, z == 3)
    spread(7, z == 0)

    def tiles(s):
        return (z + s) % 8

    def await_tile(t):
        both(ball.at[t], brecv.at[t]).wait()

    def hand_on(s, d):
        src = tiles(s)

        @pl.when(jnp.logical_and(solver, src < 2 * y))
        def _():
            for k in range(2):
                t = 2 * src + k
                await_tile(t)
                send(ball.at[t], ball.at[t], bsend, brecv.at[t], peer(d))

    hand_on(-1, 1)
    hand_on(1, -1)
    hear(True, True)
    hear(True, False)

    @pl.when(solver)
    def _():
        load_g.wait()
        for t in range(4):
            g = gbuf[:, 256 * t : 256 * t + 256]
            hi = g.astype(BF16)
            ghl[t, :256] = hi
            ghl[t, 256:] = (g - hi.astype(F32)).astype(BF16)

    own_y.wait()
    hear(False, None)

    @pl.when(core == 1)
    def _():
        signal(tok.at[2], (p - 1, col))

    for half in range(2):
        acc = jnp.zeros((16, 256), F32)
        for i, (s, e) in enumerate(zip(SPLIT, SPLIT[1:])):
            if half == 0:
                loads[i].wait()
            rows, got = pl.ds(2 * s, 2 * (e - s)), yrecv.at[2 * half + i]

            @pl.when(y // 2 == half)
            def _():
                both(h.at[rows, pl.ds(0, 7)], got).wait()

            @pl.when(y // 2 != half)
            def _():
                both(h.at[rows, pl.ds(0, 8)], got).wait()

            for t in range(s, e):
                lhs = jnp.concatenate([h[2 * t + k, 8 * half : 8 * half + 8].reshape(16, 128) for k in range(2)], axis=1)
                acc += jnp.dot(lhs, abuf[t], preferred_element_type=F32)
        part[4 * half : 4 * half + 4] = acc.reshape(4, 4, 256)

        if half == 0:

            @pl.when(core == 0)
            def _():
                pl.semaphore_wait(tok.at[2], 1)

        for k in range(4 * half, 4 * half + 4):
            to = 2 * LEVEL[k] + 1

            @pl.when(p != to)
            def _():
                send(part.at[k], pin.at[p], psem.at[0], psem.at[1], (to, col))

        if half == 0:
            hand_on(-2, 1)
            hand_on(2, -1)

    hand_on(-3, 1)

    @pl.when(solver)
    def _():
        pin[p] = part[group]
        for s in (3, 4):

            @pl.when(tiles(s) < 2 * y)
            def _():
                await_tile(2 * tiles(s))
                await_tile(2 * tiles(s) + 1)

        @pl.when(has_b)
        def _():
            await_tile(p - 1)
            own_b.wait()

        load_r.wait()
        both(pin.at[pl.ds(0, 15)], psem.at[1]).wait()
        upd[...] = r_ref[...].reshape(4, 256) - jnp.sum(pin[...], axis=0)

        for i in range(3):

            @pl.when(y > i)
            def _():
                both(xin.at[i], xrecv.at[i]).wait()
                solved = jnp.sum(xin[i], axis=0).astype(BF16)
                total = jnp.dot(solved[0], ball[4 * i], preferred_element_type=F32)
                for k in range(1, 4):
                    total += jnp.dot(solved[k], ball[4 * i + k], preferred_element_type=F32)
                upd[...] -= total

        remain = upd[...]
        low = remain - remain.astype(BF16).astype(F32)
        lhs = jnp.concatenate([remain, low], axis=0).astype(BF16)
        lhs = jnp.concatenate([lhs, lhs], axis=1)
        for t in range(4):
            res = jnp.dot(lhs, ghl[t], preferred_element_type=F32)
            gp[t] = res[:4] + res[4:]

        for j in range(1, 4):

            @pl.when(y < j)
            def _():
                for d in (2, 1, 3, 0):
                    send(gp, xin.at[y, x], xsend.at[j], xrecv.at[y], (p, 4 * j + (x + d) % 4))

        for d in (2, 1, 3):
            to = (x + d) % 4
            send(gp.at[to], oin.at[x], osem.at[0], osem.at[1], (p, 4 * y + to))
        oin[x] = gp[x]
        both(oin.at[pl.ds(0, 3)], osem.at[1]).wait()
        total = jnp.sum(oin[...], axis=0).reshape(4, 1, 256)
        ob[...] = total
        for to in (1, 0, 3, 2, 5, 4, 7, 6, 15, 14, 9, 8, 13, 12, 11, 10):

            @pl.when(p != to)
            def _():
                send(ob, o_ref.at[group], fsem.at[0], fsem.at[1], (to, col))

        o_ref[group] = total
        both(o_ref.at[pl.ds(0, 7)], fsem.at[1]).wait()

        for j in range(1, 4):

            @pl.when(y < j)
            def _():
                both(xin.at[0], xsend.at[j]).wait()

        both(oin.at[pl.ds(0, 3)], osem.at[0]).wait()
        both(pin.at[pl.ds(0, 7)], psem.at[0]).wait()
        both(pin.at[pl.ds(0, 15)], fsem.at[0]).wait()
        for s in (-1, 1, -2, 2, -3):

            @pl.when(tiles(s) < 2 * y)
            def _():
                both(ball.at[pl.ds(0, 2)], bsend).wait()

        @pl.when(has_b)
        def _():
            both(ball.at[pl.ds(0, 2)], bsend).wait()

    @pl.when(jnp.logical_not(solver))
    def _():
        both(pin.at[pl.ds(0, 8)], psem.at[0]).wait()

        @pl.when(has_b)
        def _():
            both(ball.at[pl.ds(0, 3)], bsend).wait()

        both(o_ref, fsem.at[1]).wait()

    both(h.at[:, pl.ds(0, 15)], ysend).wait()


def local(panel_pre, tail_panel, earlier, right_side, inverses):
    turns = panel_pre.shape[0]
    a = panel_pre.reshape(turns, 256, 256)
    b = tail_panel.reshape(256, 256)
    e = earlier.reshape(2, turns, 2, 128).transpose(1, 2, 0, 3).reshape(2 * turns, 2, 128)
    r = right_side.reshape(8, 4, 1, 256)
    g = inverses.reshape(256, 1024)
    dma = pltpu.SemaphoreType.DMA
    out = pl.pallas_call(
        kernel,
        out_shape=jax.ShapeDtypeStruct((8, 4, 1, 256), F32),
        in_specs=[pl.BlockSpec(memory_space=pltpu.HBM)] * 5,
        out_specs=pl.BlockSpec(memory_space=pltpu.VMEM),
        scratch_shapes=[
            pltpu.VMEM((2 * turns, 2, 128), BF16),
            pltpu.VMEM((4, 1, 256), F32),
            pltpu.VMEM((turns, 256, 256), BF16),
            pltpu.VMEM((12, 256, 256), BF16),
            pltpu.VMEM((256, 1024), F32),
            pltpu.VMEM((4, 512, 256), BF16),
            pltpu.VMEM((2 * turns, 16, 2, 128), BF16),
            pltpu.VMEM((8, 4, 256), F32),
            pltpu.VMEM((16, 4, 256), F32),
            pltpu.VMEM((4, 256), F32),
            pltpu.VMEM((4, 4, 256), F32),
            pltpu.VMEM((3, 4, 4, 4, 256), F32),
            pltpu.VMEM((4, 4, 256), F32),
            pltpu.VMEM((4, 1, 256), F32),
            dma((7,)),
            dma,
            dma((4,)),
            dma,
            dma((12,)),
            dma((2,)),
            dma((4,)),
            dma((3,)),
            dma((2,)),
            dma((2,)),
            pltpu.SemaphoreType.REGULAR((4,)),
        ],
        compiler_params=pltpu.CompilerParams(collective_id=0, has_side_effects=True, vmem_limit_bytes=64 << 20),
        cost_estimate=pl.CostEstimate(flops=2 * 32 * 256 * 256 * turns, bytes_accessed=6 << 20, transcendentals=0),
        name="solve",
    )(a, b, e, r, g)
    return out.reshape(32, 1, 1, 256)


def solution(mesh):
    in_specs = (
        P(None, "prow", None, None, "pcol", None),
        P(None, "prow", None, None, "pcol", None),
        P("pcol", None, "prow", None),
        P(None, None, "pcol", None),
        P(None, "pcol", None, None),
    )
    out_specs = P(None, None, "pcol", None)
    return jax.shard_map(local, mesh=mesh, in_specs=in_specs, out_specs=out_specs, check_vma=False)
```

```python
import jax
import jax.numpy as jnp
from jax import lax
from jax.experimental import pallas as pl
from jax.experimental.pallas import tpu as pltpu
from jax.sharding import PartitionSpec as P

MESH = pl.DeviceIdType.MESH
F32 = jnp.float32
BF16 = jnp.bfloat16
SPLIT = (0, 16, 31)
LEVEL = (4, 3, 5, 2, 0, 7, 6, 1)


def kernel(a_hbm, b_hbm, e_hbm, r_hbm, g_hbm, o_ref, e_ref, r_ref, abuf, ball, gbuf, ghl, h, part, pin, upd, gp, xin, oin, ob, lsem, ysend, yrecv, bsend, brecv, psem, xsend, xrecv, osem, fsem, tok):
    p = lax.axis_index("prow")
    col = lax.axis_index("pcol")
    z, core = p // 2, p % 2
    y, x = col // 4, col % 4
    solver = core == 1
    group = sum(jnp.where(z == level, k, 0) for k, level in enumerate(LEVEL))

    def both(ref, sem):
        return pltpu.make_async_copy(ref, ref, sem)

    def send(src, dst, ssem, rsem, to):
        pltpu.make_async_remote_copy(src, dst, ssem, rsem, device_id=to, device_id_type=MESH).start()

    load_y = pltpu.make_async_copy(e_hbm, e_ref, lsem.at[0])
    own_y = pltpu.make_async_copy(e_hbm, h.at[:, col], lsem.at[1])
    load_r = pltpu.make_async_copy(r_hbm.at[group], r_ref, lsem.at[2])
    load_g = pltpu.make_async_copy(g_hbm, gbuf, lsem.at[3])
    own_b = pltpu.make_async_copy(b_hbm, ball.at[p], lsem.at[4])
    chunks = [pl.ds(s, e - s) for s, e in zip(SPLIT, SPLIT[1:])]
    loads = [pltpu.make_async_copy(a_hbm.at[c], abuf.at[c], lsem.at[5 + i]) for i, c in enumerate(chunks)]
    has_b = p < 4 * y

    load_y.start()
    own_y.start()
    loads[0].start()

    @pl.when(solver)
    def _():
        load_g.start()
        load_r.start()

        @pl.when(has_b)
        def _():
            own_b.start()

    loads[1].start()

    def peer(d):
        return (2 * ((z + d) % 8) + 1, col)

    def signal(sem, to):
        pl.semaphore_signal(sem, inc=1, device_id=to, device_id_type=MESH)

    barrier = pltpu.get_barrier_semaphore()
    for dy in (2, 1, 3, 0):
        for dx in (2, 1, 3, 0):
            if dy or dx:
                signal(barrier, (p, (y + dy) % 4 * 4 + (x + dx) % 4))

    signal(barrier, (p + 1 - 2 * core, col))

    for d, start in ((1, 7), (7, 4)):

        @pl.when(jnp.logical_and(core == 1, z != start))
        def _():
            for k in range(2):
                signal(barrier, (2 * ((z + d) % 8) + k, col))

    load_y.wait()
    edge = jnp.logical_or(z == 0, z == 3)
    pl.semaphore_wait(barrier, jnp.where(edge, 17, 18))

    def hear(up, down):
        @pl.when(core == 1)
        def _():
            pl.semaphore_wait(tok.at[0], 1)
            if up:
                signal(tok.at[0], peer(1))
            if down is not None:
                pl.semaphore_wait(tok.at[1], 1)
            if down:
                signal(tok.at[1], peer(7))

    def first_word():
        signal(tok.at[0], peer(1))
        signal(tok.at[1], peer(7))

    for d, start in ((1, 7), (7, 4)):

        @pl.when(jnp.logical_and(core == 1, z == start))
        def _():
            signal(tok.at[3], peer(d))

    @pl.when(jnp.logical_and(core == 1, jnp.logical_not(edge)))
    def _():
        first_word()

    for yy in range(4):
        for i, (s, e) in enumerate(zip(SPLIT, SPLIT[1:])):
            rows = pl.ds(2 * s, 2 * (e - s))
            for d in (2, 1, 3, 0):
                to = (p, 4 * yy + (x + d) % 4)

                def go():
                    send(e_ref.at[rows], h.at[rows, col], ysend, yrecv.at[y // 2 * 2 + i], to)

                if d:
                    go()
                else:
                    pl.when(y != yy)(go)

    def spread(d, when):
        @pl.when(jnp.logical_and(has_b, when))
        def _():
            send(b_hbm, ball.at[p], bsend, brecv.at[p], peer(d))

    spread(1, z != 3)
    spread(7, z != 0)
    spread(0, core == 0)

    @pl.when(jnp.logical_and(core == 1, edge))
    def _():
        pl.semaphore_wait(tok.at[3], 1)
        signal(tok.at[3], (p - 1, col))
        first_word()

    @pl.when(jnp.logical_and(core == 0, edge))
    def _():
        pl.semaphore_wait(tok.at[3], 1)

    spread(1, z == 3)
    spread(7, z == 0)

    def tiles(s):
        return (z + s) % 8

    def await_tile(t):
        both(ball.at[t], brecv.at[t]).wait()

    def hand_on(s, d):
        src = tiles(s)

        @pl.when(jnp.logical_and(solver, src < 2 * y))
        def _():
            for k in range(2):
                t = 2 * src + k
                await_tile(t)
                send(ball.at[t], ball.at[t], bsend, brecv.at[t], peer(d))

    hear(True, True)
    hand_on(-1, 1)
    hand_on(1, -1)
    hear(True, False)

    @pl.when(solver)
    def _():
        load_g.wait()
        for t in range(4):
            g = gbuf[:, 256 * t : 256 * t + 256]
            hi = g.astype(BF16)
            ghl[t, :256] = hi
            ghl[t, 256:] = (g - hi.astype(F32)).astype(BF16)

    own_y.wait()
    hear(False, None)

    @pl.when(core == 1)
    def _():
        signal(tok.at[2], (p - 1, col))

    for half in range(2):
        acc = jnp.zeros((16, 256), F32)
        for i, (s, e) in enumerate(zip(SPLIT, SPLIT[1:])):
            if half == 0:
                loads[i].wait()
            rows, got = pl.ds(2 * s, 2 * (e - s)), yrecv.at[2 * half + i]

            @pl.when(y // 2 == half)
            def _():
                both(h.at[rows, pl.ds(0, 7)], got).wait()

            @pl.when(y // 2 != half)
            def _():
                both(h.at[rows, pl.ds(0, 8)], got).wait()

            for t in range(s, e):
                lhs = jnp.concatenate([h[2 * t + k, 8 * half : 8 * half + 8].reshape(16, 128) for k in range(2)], axis=1)
                acc += jnp.dot(lhs, abuf[t], preferred_element_type=F32)
        part[4 * half : 4 * half + 4] = acc.reshape(4, 4, 256)

        if half == 0:

            @pl.when(core == 0)
            def _():
                pl.semaphore_wait(tok.at[2], 1)

        for k in range(4 * half, 4 * half + 4):
            to = 2 * LEVEL[k] + 1

            @pl.when(p != to)
            def _():
                send(part.at[k], pin.at[p], psem.at[0], psem.at[1], (to, col))

        if half == 0:
            hand_on(-2, 1)
            hand_on(2, -1)

    hand_on(-3, 1)

    @pl.when(solver)
    def _():
        pin[p] = part[group]
        for s in (3, 4):

            @pl.when(tiles(s) < 2 * y)
            def _():
                await_tile(2 * tiles(s))
                await_tile(2 * tiles(s) + 1)

        @pl.when(has_b)
        def _():
            await_tile(p - 1)
            own_b.wait()

        load_r.wait()
        both(pin.at[pl.ds(0, 15)], psem.at[1]).wait()
        upd[...] = r_ref[...].reshape(4, 256) - jnp.sum(pin[...], axis=0)

        for i in range(3):

            @pl.when(y > i)
            def _():
                both(xin.at[i], xrecv.at[i]).wait()
                solved = jnp.sum(xin[i], axis=0).astype(BF16)
                total = jnp.dot(solved[0], ball[4 * i], preferred_element_type=F32)
                for k in range(1, 4):
                    total += jnp.dot(solved[k], ball[4 * i + k], preferred_element_type=F32)
                upd[...] -= total

        remain = upd[...]
        low = remain - remain.astype(BF16).astype(F32)
        lhs = jnp.concatenate([remain, low], axis=0).astype(BF16)
        lhs = jnp.concatenate([lhs, lhs], axis=1)
        for t in range(4):
            res = jnp.dot(lhs, ghl[t], preferred_element_type=F32)
            gp[t] = res[:4] + res[4:]

        for j in range(1, 4):

            @pl.when(y < j)
            def _():
                for d in (2, 1, 3, 0):
                    send(gp, xin.at[y, x], xsend.at[j], xrecv.at[y], (p, 4 * j + (x + d) % 4))

        for d in (2, 1, 3):
            to = (x + d) % 4
            send(gp.at[to], oin.at[x], osem.at[0], osem.at[1], (p, 4 * y + to))
        oin[x] = gp[x]
        both(oin.at[pl.ds(0, 3)], osem.at[1]).wait()
        total = jnp.sum(oin[...], axis=0).reshape(4, 1, 256)
        ob[...] = total
        for to in (1, 0, 3, 2, 5, 4, 7, 6, 15, 14, 9, 8, 13, 12, 11, 10):

            @pl.when(p != to)
            def _():
                send(ob, o_ref.at[group], fsem.at[0], fsem.at[1], (to, col))

        o_ref[group] = total
        both(o_ref.at[pl.ds(0, 7)], fsem.at[1]).wait()

        for j in range(1, 4):

            @pl.when(y < j)
            def _():
                both(xin.at[0], xsend.at[j]).wait()

        both(oin.at[pl.ds(0, 3)], osem.at[0]).wait()
        both(pin.at[pl.ds(0, 7)], psem.at[0]).wait()
        both(pin.at[pl.ds(0, 15)], fsem.at[0]).wait()
        for s in (-1, 1, -2, 2, -3):

            @pl.when(tiles(s) < 2 * y)
            def _():
                both(ball.at[pl.ds(0, 2)], bsend).wait()

        @pl.when(has_b)
        def _():
            both(ball.at[pl.ds(0, 2)], bsend).wait()

    @pl.when(jnp.logical_not(solver))
    def _():
        both(pin.at[pl.ds(0, 8)], psem.at[0]).wait()

        @pl.when(has_b)
        def _():
            both(ball.at[pl.ds(0, 3)], bsend).wait()

        both(o_ref, fsem.at[1]).wait()

    both(h.at[:, pl.ds(0, 15)], ysend).wait()


def local(panel_pre, tail_panel, earlier, right_side, inverses):
    turns = panel_pre.shape[0]
    a = panel_pre.reshape(turns, 256, 256)
    b = tail_panel.reshape(256, 256)
    e = earlier.reshape(2, turns, 2, 128).transpose(1, 2, 0, 3).reshape(2 * turns, 2, 128)
    r = right_side.reshape(8, 4, 1, 256)
    g = inverses.reshape(256, 1024)
    dma = pltpu.SemaphoreType.DMA
    out = pl.pallas_call(
        kernel,
        out_shape=jax.ShapeDtypeStruct((8, 4, 1, 256), F32),
        in_specs=[pl.BlockSpec(memory_space=pltpu.HBM)] * 5,
        out_specs=pl.BlockSpec(memory_space=pltpu.VMEM),
        scratch_shapes=[
            pltpu.VMEM((2 * turns, 2, 128), BF16),
            pltpu.VMEM((4, 1, 256), F32),
            pltpu.VMEM((turns, 256, 256), BF16),
            pltpu.VMEM((12, 256, 256), BF16),
            pltpu.VMEM((256, 1024), F32),
            pltpu.VMEM((4, 512, 256), BF16),
            pltpu.VMEM((2 * turns, 16, 2, 128), BF16),
            pltpu.VMEM((8, 4, 256), F32),
            pltpu.VMEM((16, 4, 256), F32),
            pltpu.VMEM((4, 256), F32),
            pltpu.VMEM((4, 4, 256), F32),
            pltpu.VMEM((3, 4, 4, 4, 256), F32),
            pltpu.VMEM((4, 4, 256), F32),
            pltpu.VMEM((4, 1, 256), F32),
            dma((7,)),
            dma,
            dma((4,)),
            dma,
            dma((12,)),
            dma((2,)),
            dma((4,)),
            dma((3,)),
            dma((2,)),
            dma((2,)),
            pltpu.SemaphoreType.REGULAR((4,)),
        ],
        compiler_params=pltpu.CompilerParams(collective_id=0, has_side_effects=True, vmem_limit_bytes=64 << 20),
        cost_estimate=pl.CostEstimate(flops=2 * 32 * 256 * 256 * turns, bytes_accessed=6 << 20, transcendentals=0),
        name="solve",
    )(a, b, e, r, g)
    return out.reshape(32, 1, 1, 256)


def solution(mesh):
    in_specs = (
        P(None, "prow", None, None, "pcol", None),
        P(None, "prow", None, None, "pcol", None),
        P("pcol", None, "prow", None),
        P(None, None, "pcol", None),
        P(None, "pcol", None, None),
    )
    out_specs = P(None, None, "pcol", None)
    return jax.shard_map(local, mesh=mesh, in_specs=in_specs, out_specs=out_specs, check_vma=False)
```

```python
import jax
import jax.numpy as jnp
from jax import lax
from jax.experimental import pallas as pl
from jax.experimental.pallas import tpu as pltpu
from jax.sharding import PartitionSpec as P

MESH = pl.DeviceIdType.MESH
F32 = jnp.float32
BF16 = jnp.bfloat16
SPLIT = (0, 16, 31)
LEVEL = (4, 3, 5, 2, 0, 7, 6, 1)


def kernel(a_hbm, b_hbm, e_hbm, r_hbm, g_hbm, o_ref, e_ref, r_ref, abuf, ball, gbuf, ghl, h, part, pin, upd, gp, xin, oin, ob, lsem, ysend, yrecv, bsend, brecv, psem, xsend, xrecv, osem, fsem, tok):
    p = lax.axis_index("prow")
    col = lax.axis_index("pcol")
    z, core = p // 2, p % 2
    y, x = col // 4, col % 4
    solver = core == 1
    group = sum(jnp.where(z == level, k, 0) for k, level in enumerate(LEVEL))

    def both(ref, sem):
        return pltpu.make_async_copy(ref, ref, sem)

    def send(src, dst, ssem, rsem, to):
        pltpu.make_async_remote_copy(src, dst, ssem, rsem, device_id=to, device_id_type=MESH).start()

    load_y = pltpu.make_async_copy(e_hbm, e_ref, lsem.at[0])
    own_y = pltpu.make_async_copy(e_hbm, h.at[:, col], lsem.at[1])
    load_r = pltpu.make_async_copy(r_hbm.at[group], r_ref, lsem.at[2])
    load_g = pltpu.make_async_copy(g_hbm, gbuf, lsem.at[3])
    own_b = pltpu.make_async_copy(b_hbm, ball.at[p], lsem.at[4])
    chunks = [pl.ds(s, e - s) for s, e in zip(SPLIT, SPLIT[1:])]
    loads = [pltpu.make_async_copy(a_hbm.at[c], abuf.at[c], lsem.at[5 + i]) for i, c in enumerate(chunks)]
    has_b = p < 4 * y

    load_y.start()
    own_y.start()
    loads[0].start()

    @pl.when(solver)
    def _():
        load_g.start()
        load_r.start()

        @pl.when(has_b)
        def _():
            own_b.start()

    loads[1].start()

    def peer(d):
        return (2 * ((z + d) % 8) + 1, col)

    def signal(sem, to):
        pl.semaphore_signal(sem, inc=1, device_id=to, device_id_type=MESH)

    barrier = pltpu.get_barrier_semaphore()
    for dy in (2, 1, 3, 0):
        for dx in (2, 1, 3, 0):
            if dy or dx:
                signal(barrier, (p, (y + dy) % 4 * 4 + (x + dx) % 4))

    signal(barrier, (p + 1 - 2 * core, col))

    for d, start in ((1, 7), (7, 4)):

        @pl.when(jnp.logical_and(core == 1, z != start))
        def _():
            for k in range(2):
                signal(barrier, (2 * ((z + d) % 8) + k, col))

    load_y.wait()
    edge = jnp.logical_or(z == 0, z == 3)
    pl.semaphore_wait(barrier, jnp.where(edge, 17, 18))

    def hear(up, down):
        @pl.when(core == 1)
        def _():
            pl.semaphore_wait(tok.at[0], 1)
            if up:
                signal(tok.at[0], peer(1))
            if down is not None:
                pl.semaphore_wait(tok.at[1], 1)
            if down:
                signal(tok.at[1], peer(7))

    def first_word():
        signal(tok.at[0], peer(1))
        signal(tok.at[1], peer(7))

    for d, start in ((1, 7), (7, 4)):

        @pl.when(jnp.logical_and(core == 1, z == start))
        def _():
            signal(tok.at[3], peer(d))

    @pl.when(jnp.logical_and(core == 1, jnp.logical_not(edge)))
    def _():
        first_word()

    for yy in range(4):
        for i, (s, e) in enumerate(zip(SPLIT, SPLIT[1:])):
            rows = pl.ds(2 * s, 2 * (e - s))
            for d in (2, 1, 3, 0):
                to = (p, 4 * yy + (x + d) % 4)

                def go():
                    send(e_ref.at[rows], h.at[rows, col], ysend, yrecv.at[y // 2 * 2 + i], to)

                if d:
                    go()
                else:
                    pl.when(y != yy)(go)

    def spread(d, when):
        @pl.when(jnp.logical_and(has_b, when))
        def _():
            send(b_hbm, ball.at[p], bsend, brecv.at[p], peer(d))

    spread(1, z != 3)
    spread(7, z != 0)
    spread(0, core == 0)

    @pl.when(jnp.logical_and(core == 1, edge))
    def _():
        pl.semaphore_wait(tok.at[3], 1)
        signal(tok.at[3], (p - 1, col))
        first_word()

    @pl.when(jnp.logical_and(core == 0, edge))
    def _():
        pl.semaphore_wait(tok.at[3], 1)

    spread(1, z == 3)
    spread(7, z == 0)

    def tiles(s):
        return (z + s) % 8

    def await_tile(t):
        both(ball.at[t], brecv.at[t]).wait()

    def hand_on(s, d):
        src = tiles(s)

        @pl.when(jnp.logical_and(solver, src < 2 * y))
        def _():
            for k in range(2):
                t = 2 * src + k
                await_tile(t)
                send(ball.at[t], ball.at[t], bsend, brecv.at[t], peer(d))

    hear(True, True)
    hand_on(-1, 1)
    hand_on(1, -1)
    hear(True, False)

    @pl.when(solver)
    def _():
        load_g.wait()
        for t in range(4):
            g = gbuf[:, 256 * t : 256 * t + 256]
            hi = g.astype(BF16)
            ghl[t, :256] = hi
            ghl[t, 256:] = (g - hi.astype(F32)).astype(BF16)

    own_y.wait()
    hear(False, None)

    @pl.when(core == 1)
    def _():
        signal(tok.at[2], (p - 1, col))

    for half in range(2):
        acc = jnp.zeros((16, 256), F32)
        for i, (s, e) in enumerate(zip(SPLIT, SPLIT[1:])):
            if half == 0:
                loads[i].wait()
            rows, got = pl.ds(2 * s, 2 * (e - s)), yrecv.at[2 * half + i]

            @pl.when(y // 2 == half)
            def _():
                both(h.at[rows, pl.ds(0, 7)], got).wait()

            @pl.when(y // 2 != half)
            def _():
                both(h.at[rows, pl.ds(0, 8)], got).wait()

            for t in range(s, e):
                lhs = jnp.concatenate([h[2 * t + k, 8 * half : 8 * half + 8].reshape(16, 128) for k in range(2)], axis=1)
                acc += jnp.dot(lhs, abuf[t], preferred_element_type=F32)
        part[4 * half : 4 * half + 4] = acc.reshape(4, 4, 256)

        if half == 0:

            @pl.when(core == 0)
            def _():
                pl.semaphore_wait(tok.at[2], 1)

        for k in ((0, 2, 1, 3), (7, 4, 5, 6))[half]:
            to = 2 * LEVEL[k] + 1

            @pl.when(p != to)
            def _():
                send(part.at[k], pin.at[p], psem.at[0], psem.at[1], (to, col))

        if half == 0:
            hand_on(-2, 1)
            hand_on(2, -1)

    hand_on(-3, 1)

    @pl.when(solver)
    def _():
        pin[p] = part[group]
        for s in (3, 4):

            @pl.when(tiles(s) < 2 * y)
            def _():
                await_tile(2 * tiles(s))
                await_tile(2 * tiles(s) + 1)

        @pl.when(has_b)
        def _():
            await_tile(p - 1)
            own_b.wait()

        load_r.wait()
        both(pin.at[pl.ds(0, 15)], psem.at[1]).wait()
        upd[...] = r_ref[...].reshape(4, 256) - jnp.sum(pin[...], axis=0)

        for i in range(3):

            @pl.when(y > i)
            def _():
                both(xin.at[i], xrecv.at[i]).wait()
                solved = jnp.sum(xin[i], axis=0).astype(BF16)
                total = jnp.dot(solved[0], ball[4 * i], preferred_element_type=F32)
                for k in range(1, 4):
                    total += jnp.dot(solved[k], ball[4 * i + k], preferred_element_type=F32)
                upd[...] -= total

        remain = upd[...]
        low = remain - remain.astype(BF16).astype(F32)
        lhs = jnp.concatenate([remain, low], axis=0).astype(BF16)
        lhs = jnp.concatenate([lhs, lhs], axis=1)
        for t in range(4):
            res = jnp.dot(lhs, ghl[t], preferred_element_type=F32)
            gp[t] = res[:4] + res[4:]

        for j in range(1, 4):

            @pl.when(y < j)
            def _():
                for d in (2, 1, 3, 0):
                    send(gp, xin.at[y, x], xsend.at[j], xrecv.at[y], (p, 4 * j + (x + d) % 4))

        for d in (2, 1, 3):
            to = (x + d) % 4
            send(gp.at[to], oin.at[x], osem.at[0], osem.at[1], (p, 4 * y + to))
        oin[x] = gp[x]
        both(oin.at[pl.ds(0, 3)], osem.at[1]).wait()
        total = jnp.sum(oin[...], axis=0).reshape(4, 1, 256)
        ob[...] = total
        for to in (1, 0, 3, 2, 5, 4, 7, 6, 15, 14, 9, 8, 13, 12, 11, 10):

            @pl.when(p != to)
            def _():
                send(ob, o_ref.at[group], fsem.at[0], fsem.at[1], (to, col))

        o_ref[group] = total
        both(o_ref.at[pl.ds(0, 7)], fsem.at[1]).wait()

        for j in range(1, 4):

            @pl.when(y < j)
            def _():
                both(xin.at[0], xsend.at[j]).wait()

        both(oin.at[pl.ds(0, 3)], osem.at[0]).wait()
        both(pin.at[pl.ds(0, 7)], psem.at[0]).wait()
        both(pin.at[pl.ds(0, 15)], fsem.at[0]).wait()
        for s in (-1, 1, -2, 2, -3):

            @pl.when(tiles(s) < 2 * y)
            def _():
                both(ball.at[pl.ds(0, 2)], bsend).wait()

        @pl.when(has_b)
        def _():
            both(ball.at[pl.ds(0, 2)], bsend).wait()

    @pl.when(jnp.logical_not(solver))
    def _():
        both(pin.at[pl.ds(0, 8)], psem.at[0]).wait()

        @pl.when(has_b)
        def _():
            both(ball.at[pl.ds(0, 3)], bsend).wait()

        both(o_ref, fsem.at[1]).wait()

    both(h.at[:, pl.ds(0, 15)], ysend).wait()


def local(panel_pre, tail_panel, earlier, right_side, inverses):
    turns = panel_pre.shape[0]
    a = panel_pre.reshape(turns, 256, 256)
    b = tail_panel.reshape(256, 256)
    e = earlier.reshape(2, turns, 2, 128).transpose(1, 2, 0, 3).reshape(2 * turns, 2, 128)
    r = right_side.reshape(8, 4, 1, 256)
    g = inverses.reshape(256, 1024)
    dma = pltpu.SemaphoreType.DMA
    out = pl.pallas_call(
        kernel,
        out_shape=jax.ShapeDtypeStruct((8, 4, 1, 256), F32),
        in_specs=[pl.BlockSpec(memory_space=pltpu.HBM)] * 5,
        out_specs=pl.BlockSpec(memory_space=pltpu.VMEM),
        scratch_shapes=[
            pltpu.VMEM((2 * turns, 2, 128), BF16),
            pltpu.VMEM((4, 1, 256), F32),
            pltpu.VMEM((turns, 256, 256), BF16),
            pltpu.VMEM((12, 256, 256), BF16),
            pltpu.VMEM((256, 1024), F32),
            pltpu.VMEM((4, 512, 256), BF16),
            pltpu.VMEM((2 * turns, 16, 2, 128), BF16),
            pltpu.VMEM((8, 4, 256), F32),
            pltpu.VMEM((16, 4, 256), F32),
            pltpu.VMEM((4, 256), F32),
            pltpu.VMEM((4, 4, 256), F32),
            pltpu.VMEM((3, 4, 4, 4, 256), F32),
            pltpu.VMEM((4, 4, 256), F32),
            pltpu.VMEM((4, 1, 256), F32),
            dma((7,)),
            dma,
            dma((4,)),
            dma,
            dma((12,)),
            dma((2,)),
            dma((4,)),
            dma((3,)),
            dma((2,)),
            dma((2,)),
            pltpu.SemaphoreType.REGULAR((4,)),
        ],
        compiler_params=pltpu.CompilerParams(collective_id=0, has_side_effects=True, vmem_limit_bytes=64 << 20),
        cost_estimate=pl.CostEstimate(flops=2 * 32 * 256 * 256 * turns, bytes_accessed=6 << 20, transcendentals=0),
        name="solve",
    )(a, b, e, r, g)
    return out.reshape(32, 1, 1, 256)


def solution(mesh):
    in_specs = (
        P(None, "prow", None, None, "pcol", None),
        P(None, "prow", None, None, "pcol", None),
        P("pcol", None, "prow", None),
        P(None, None, "pcol", None),
        P(None, "pcol", None, None),
    )
    out_specs = P(None, None, "pcol", None)
    return jax.shard_map(local, mesh=mesh, in_specs=in_specs, out_specs=out_specs, check_vma=False)
```
